128 devices in a mesh: tm: 32 (over x_lo, z, y), guide: 4 (over x_hi, core).
Axes of the slice: x: 4 (x_hi: 2, x_lo: 2; x = x_hi * 2 + x_lo), y: 4, z: 4, core: 2. Of those that a mesh axis runs over, the one named last changes fastest.
Arguments:
- hidden_rows: bfloat16 [4, 24576, 1024], P('guide', 'tm'), may hold values from -6 to 6
- modulation: float32 [4, 3, 1024], P('guide'), may hold values from -3 to 3
- project_in: bfloat16 [1024, 3072], replicated, may hold values from -0.1875 to 0.1875
- project_out: bfloat16 [1024, 1024], replicated, may hold values from -0.1875 to 0.1875
- to_vocoder: bfloat16 [1024, 384], replicated, may hold values from -0.1875 to 0.1875
- upsample_taps: bfloat16 [4, 384, 192], replicated, may hold values from -0.21875 to 0.21875
- snake_alpha: float32 [192], replicated, may hold values from 0.2 to 3
- guidance: float32 [2], replicated, may hold values from 1 to 3
- branch_ids: int32 [4], replicated, may hold values from 0 to 1, as said below
Outputs:
- wave_features: bfloat16 [384, 49152], P('guide', 'tm')
The draws below stay inside these ranges and needn't reach their ends.
Inputs may be any that keep to these rules, and one draw needn't show every extreme that they name: `branch_ids`: rows 2s and 2s + 1 hold one 0 and one 1, for every stream s.
All inputs are finite; a program needn't handle non-finite values.
Results may differ from the reference program's by a relative error of at most 0.015.
Values may be sent and summed in bfloat16 or wider, within the bound.
A program may use at most 128 MiB of HBM per device.

```python
import math
import jax
import jax.numpy as jnp
from jax import lax

D = 1024
HEADS = 16
BLOCK = 48
CIN = 384
COUT = 192
FR_DEV = 768
ROWS = 4
STREAMS = 2
FRAMES = 24576
N_TM = 32


def draw_branch_ids(key, part):
    key = jax.random.fold_in(key, 7)
    leading = jax.random.randint(key, (STREAMS,), 0, 2, dtype=jnp.int32)
    return jnp.stack([leading, 1 - leading], axis=1).reshape(ROWS)


def block_levels(key, extent, shards, low, largest):
    factor_of = 1.0
    for axis_at, shards_of in shards:
        heights = jax.random.uniform(jax.random.fold_in(jax.random.fold_in(key, 6), axis_at), (shards_of,), jnp.float32, low / len(shards), largest / len(shards))
        factor_of = factor_of * jnp.repeat(jnp.exp(heights), extent[axis_at] // shards_of).reshape((-1,) + (1,) * (len(extent) - 1 - axis_at))
    return factor_of


def gaussian(key, extent, spread, reach, split=(), held_as=jnp.bfloat16):
    level = block_levels(key, extent, split, -0.22, 0.18) if split else 1.0
    drawn = jax.random.normal(key, extent, jnp.float32) * spread * level
    return jnp.minimum(jnp.maximum(drawn, -reach), reach).astype(held_as)


def setup_inputs(seed: int = 0) -> dict:
    streams_of = jax.random.split(jax.random.key(seed), 10)
    hidden_rows = gaussian(streams_of[0], (ROWS, FRAMES, D), 1.0, 6.0, ((0, 4), (1, 32)))
    modulation = gaussian(streams_of[1], (ROWS, 3, D), 0.5, 3.0, ((0, 4),), jnp.float32)
    project_in = gaussian(streams_of[2], (D, 3 * D), D ** -0.5, 0.1875)
    project_out = gaussian(streams_of[3], (D, D), D ** -0.5, 0.1875)
    to_vocoder = gaussian(streams_of[4], (D, CIN), D ** -0.5, 0.1875)
    upsample_taps = gaussian(streams_of[5], (4, CIN, COUT), (2 * CIN) ** -0.5, 0.21875)
    snake_alpha = jnp.clip(jnp.exp(jax.random.uniform(streams_of[6], (COUT,), jnp.float32, math.log(0.2), math.log(3.0))), 0.2, 3.0)
    guidance = jnp.clip(jax.random.uniform(streams_of[7], (STREAMS,), jnp.float32, 1.0, 3.0), 1.0, 3.0)
    branch_ids = draw_branch_ids(jax.random.fold_in(streams_of[9], 71), 0)
    return dict(hidden_rows=hidden_rows, modulation=modulation, project_in=project_in, project_out=project_out, to_vocoder=to_vocoder, upsample_taps=upsample_taps, snake_alpha=snake_alpha, guidance=guidance, branch_ids=branch_ids)


HALF_BAND = (3.0 / 256.0, -25.0 / 256.0, 150.0 / 256.0, 150.0 / 256.0, -25.0 / 256.0, 3.0 / 256.0)
LOW_PASS = (0.012, -0.06, 0.3, 0.3, -0.06, 0.012)
CENTER_TAP = 0.5

def modulated(rows_in, scale_row, shift_row):
    widened = rows_in.astype(jnp.float32)
    centered = widened - lax.optimization_barrier(jnp.mean(widened, axis=-1, keepdims=True))
    variance = lax.optimization_barrier(jnp.mean(centered * centered, axis=-1, keepdims=True))
    normed = centered * lax.rsqrt(variance + 1e-06)
    return (normed * (1.0 + scale_row) + shift_row).astype(jnp.bfloat16)

def block_attend(queries, extended, usable, head_count, block):
    frames = queries.shape[0]
    model_width = queries.shape[1]
    head_size = model_width // head_count
    count = frames // block
    query_blocks = queries.reshape(count, block, head_count, head_size).astype(jnp.float32)
    pieces = [extended[j * block:j * block + frames].reshape(count, block, 2 * model_width) for j in range(4)]
    key_rows = jnp.concatenate(pieces, axis=1)
    key_heads = key_rows[:, :, :model_width].reshape(count, 4 * block, head_count, head_size).astype(jnp.float32)
    value_heads = key_rows[:, :, model_width:].reshape(count, 4 * block, head_count, head_size).astype(jnp.float32)
    scores = jnp.einsum('nqhd,nkhd->nhqk', query_blocks, key_heads) * (1.0 / math.sqrt(head_size))
    scores = jnp.where(usable[:, None, None, :], scores, -jnp.inf)
    row_max = lax.optimization_barrier(jnp.max(scores, axis=3, keepdims=True))
    raised = jnp.exp(scores - row_max)
    weights = (raised / lax.optimization_barrier(jnp.sum(raised, axis=3, keepdims=True))).astype(jnp.bfloat16)
    result = jnp.einsum('nhqk,nkhd->nqhd', weights.astype(jnp.float32), value_heads)
    return result.astype(jnp.bfloat16).reshape(frames, model_width)

def channel_mix(weight, signal):
    return lax.dot_general(weight, signal, (((0,), (0,)), ((), ())), preferred_element_type=jnp.float32)

def upsample(window, tap_table):
    span = window.shape[1] - 2
    even_part = channel_mix(tap_table[1], window[:, 1:span + 1]) + channel_mix(tap_table[3], window[:, 0:span])
    odd_part = channel_mix(tap_table[0], window[:, 2:span + 2]) + channel_mix(tap_table[2], window[:, 1:span + 1])
    return jnp.stack([even_part, odd_part], axis=2).reshape(even_part.shape[0], 2 * span)

def periodic(values, snake_rate):
    return values + jnp.square(jnp.sin(snake_rate * values)) / snake_rate

def activate(extended, snake_rate, odd_usable):
    span = extended.shape[1] - 10
    odd_edge = HALF_BAND[0] * extended[:, 0:span + 5]
    for offset in range(1, 6):
        odd_edge = odd_edge + HALF_BAND[offset] * extended[:, offset:offset + span + 5]
    odd_edge = jnp.where(odd_usable[None, :], periodic(odd_edge, snake_rate), 0.0)
    result = CENTER_TAP * periodic(extended[:, 5:5 + span], snake_rate)
    for offset in range(6):
        result = result + LOW_PASS[offset] * odd_edge[:, offset:offset + span]
    return result

def reference(hidden_rows, modulation, project_in, project_out, to_vocoder, upsample_taps, snake_alpha, guidance, branch_ids):
    normed = modulated(hidden_rows, modulation[:, 0][:, None, :], modulation[:, 1][:, None, :])
    projections = jnp.dot(normed.reshape(ROWS * FRAMES, D), project_in, preferred_element_type=jnp.float32)
    projections = projections.astype(jnp.bfloat16).reshape(ROWS, FRAMES, 3 * D)
    queries = projections[:, :, :D]
    key_value = projections[:, :, D:]
    padded = jnp.pad(key_value, ((0, 0), (2 * BLOCK, BLOCK), (0, 0)))
    local_blocks = FR_DEV // BLOCK
    total_blocks = FRAMES // BLOCK

    def window_run(flat_index):
        row_index = (flat_index // N_TM).astype(jnp.int32)
        run_index = (flat_index % N_TM).astype(jnp.int32)
        start = (run_index * FR_DEV).astype(jnp.int32)
        query_run = lax.dynamic_slice(queries, (row_index, start, jnp.int32(0)), (1, FR_DEV, D))[0]
        extended = lax.dynamic_slice(padded, (row_index, start, jnp.int32(0)), (1, FR_DEV + 3 * BLOCK, 2 * D))[0]
        block_ids = run_index * local_blocks + jnp.arange(local_blocks, dtype=jnp.int32)
        key_ids = block_ids[:, None] - 2 + (jnp.arange(4 * BLOCK, dtype=jnp.int32) // BLOCK)[None, :]
        usable = (key_ids >= 0) & (key_ids < total_blocks)
        return block_attend(query_run, extended, usable, HEADS, BLOCK)
    attended = lax.map(window_run, jnp.arange(ROWS * N_TM, dtype=jnp.int32)).reshape(ROWS, FRAMES, D)
    mixed_out = jnp.dot(attended.reshape(ROWS * FRAMES, D), project_out, preferred_element_type=jnp.float32)
    mixed_out = mixed_out.reshape(ROWS, FRAMES, D)
    updated = (hidden_rows.astype(jnp.float32) + modulation[:, 2][:, None, :] * mixed_out).astype(jnp.bfloat16)
    projected = jnp.dot(updated.reshape(ROWS * FRAMES, D), to_vocoder, preferred_element_type=jnp.float32)
    projected = projected.reshape(ROWS, FRAMES, CIN).transpose(0, 2, 1)
    grouped = projected.reshape(STREAMS, 2, CIN, FRAMES)
    cond_first = (branch_ids.reshape(STREAMS, 2)[:, 0] == 0)[:, None, None]
    cond_rows = jnp.where(cond_first, grouped[:, 0], grouped[:, 1])
    uncond_rows = jnp.where(cond_first, grouped[:, 1], grouped[:, 0])
    guided = (uncond_rows + guidance[:, None, None] * (cond_rows - uncond_rows)).astype(jnp.bfloat16)
    snake_rate = snake_alpha[:, None]
    all_frames = 2 * FRAMES
    positions = jnp.arange(all_frames + 5, dtype=jnp.int32) - 3
    odd_usable = (positions >= 0) & (positions < all_frames)

    def vocode(mel_frames):
        window = jnp.pad(mel_frames, ((0, 0), (1, 1)))
        upsampled = upsample(window, upsample_taps)
        extended = jnp.pad(upsampled, ((0, 0), (5, 5)))
        return activate(extended, snake_rate, odd_usable).astype(jnp.bfloat16)
    waves = lax.map(vocode, guided)
    return waves.reshape(STREAMS * COUT, all_frames)
```

```python
import functools
import math

import jax
import jax.numpy as jnp
from jax import lax
from jax.experimental import pallas as pl
from jax.experimental.pallas import tpu as pltpu
from jax.sharding import PartitionSpec as P

HEADS = 16
BLOCK = 48
HALF_BAND = (3.0 / 256.0, -25.0 / 256.0, 150.0 / 256.0, 150.0 / 256.0, -25.0 / 256.0, 3.0 / 256.0)
LOW_PASS = (0.012, -0.06, 0.3, 0.3, -0.06, 0.012)
CENTER_TAP = 0.5
SIN2 = (9.869604202977849, -32.469663586217976, 42.72706432039706,
        -30.100639734504547, 13.048356860034854, -3.3563323291898937)
MASKED = -1e30
MESH = pl.DeviceIdType.MESH
F32 = jnp.float32
BF16 = jnp.bfloat16

PAIR = 2 * BLOCK
LEFT = 2 * BLOCK
RIM = 16


def nt_dot(a, b):
    return lax.dot_general(a, b, (((1,), (1,)), ((), ())), preferred_element_type=F32)


def dot(a, b):
    return jnp.dot(a, b, preferred_element_type=F32)


def kernel(n_tm, hidden, modulation, w_in_hbm, w_out_hbm, w_voc_hbm, taps_hbm, alpha_hbm,
           guidance, branch_ids, out,
           hid, normed, w_in, w_out, w_voc, taps, mod, alpha,
           q_buf, k_buf, v_buf, att, upd, own, par, guided, y_buf, wave, taps_t, perm,
           win_sem, in_sem, send_sem, recv_sem):
    frames = hidden.shape[1]
    width = hidden.shape[2]
    pairs = frames // PAIR
    groups = width // 128
    extent = LEFT + frames + BLOCK
    half = out.shape[0]
    lanes = own.shape[0]
    cin = own.shape[1]
    total_frames = n_tm * frames

    tm = lax.axis_index("tm")
    member = lax.axis_index("guide")
    parity = lax.rem(member, 2)
    other = member + 1 - 2 * parity
    right_tm = lax.rem(tm + 1, n_tm)
    left_tm = lax.rem(tm + n_tm - 1, n_tm)
    left, right = (left_tm, member), (right_tm, member)
    partner = (tm, other)
    left_partner, right_partner = (left_tm, other), (right_tm, other)

    def load(src, dst, sem):
        copy = pltpu.make_async_copy(src, dst, sem)
        copy.start()
        return copy

    hid_copy = load(hidden.at[0], hid.at[pl.ds(LEFT, frames)], in_sem.at[0])
    mod_copy = load(modulation.at[:, 0], mod, in_sem.at[1])
    tiles = w_in.shape[0]
    win_copies = [load(w_in_hbm.at[:, pl.ds(256 * j, 256)], w_in.at[j], win_sem.at[j])
                  for j in range(tiles)]
    taps_copy = load(taps_hbm, taps, in_sem.at[2])
    alpha_copy = load(alpha_hbm, alpha, in_sem.at[3])
    wout_copy = load(w_out_hbm, w_out, in_sem.at[4])
    wvoc_copy = load(w_voc_hbm, w_voc, in_sem.at[5])

    barrier = pltpu.get_barrier_semaphore()
    for device in (left, right, partner, left_partner, right_partner):
        pl.semaphore_signal(barrier, inc=1, device_id=device, device_id_type=MESH)

    def send(i, src, dst, device):
        copy = pltpu.make_async_remote_copy(
            src_ref=src, dst_ref=dst, send_sem=send_sem.at[i], recv_sem=recv_sem.at[i],
            device_id=device, device_id_type=MESH)
        copy.start()
        return copy

    pl.semaphore_wait(barrier, 5)
    to_right = send(0, hidden.at[0, pl.ds(frames - LEFT, LEFT)], hid.at[pl.ds(0, LEFT)], right)
    to_left = send(1, hidden.at[0, pl.ds(0, BLOCK)], hid.at[pl.ds(LEFT + frames, BLOCK)], left)

    spare = k_buf.shape[1] - extent
    k_buf[:, pl.ds(extent, spare), :] = jnp.zeros((groups, spare, 128), BF16)
    v_buf[:, pl.ds(extent, spare), :] = jnp.zeros((groups, spare, 128), BF16)
    gap = lanes - frames - 2 * RIM
    own[pl.ds(frames + RIM, gap), :] = jnp.zeros((gap, cin), BF16)
    par[pl.ds(frames + RIM, gap), :] = jnp.zeros((gap, cin), BF16)
    row = lax.broadcasted_iota(jnp.int32, (256, 256), 0)
    col = lax.broadcasted_iota(jnp.int32, (256, 256), 1)
    perm[...] = jnp.where(row == (col % 2) * 128 + col // 2, 1.0, 0.0).astype(BF16)

    mod_copy.wait()
    scale_row = 1.0 + mod[0:1, :]
    shift_row = mod[1:2, :]

    def normalise(start, rows):
        x = hid[pl.ds(start, rows), :].astype(F32)
        centered = x - jnp.mean(x, axis=-1, keepdims=True)
        variance = jnp.mean(centered * centered, axis=-1, keepdims=True)
        result = centered * lax.rsqrt(variance + 1e-6) * scale_row + shift_row
        normed[pl.ds(start, rows), :] = result.astype(BF16)

    hid_copy.wait()

    def norm_step(i, carry):
        normalise(pl.multiple_of(LEFT + i * BLOCK, BLOCK), BLOCK)
        return carry

    lax.fori_loop(0, frames // BLOCK, norm_step, 0)

    per = groups // 2
    local = pl.ds(LEFT, frames)

    def q_step(j, carry):
        pltpu.make_async_copy(w_in.at[j], w_in.at[j], win_sem.at[j]).wait()
        acc = dot(normed[local, :], w_in[j]) * (math.log2(math.e) / math.sqrt(width // HEADS))
        acc = acc.astype(BF16)
        q_buf[2 * j] = acc[:, :128]
        q_buf[2 * j + 1] = acc[:, 128:]
        return carry

    lax.fori_loop(0, per, q_step, 0)

    def kv_local(base, buf):
        def step(j, carry):
            pltpu.make_async_copy(w_in.at[base + j], w_in.at[base + j], win_sem.at[base + j]).wait()
            acc = dot(normed[local, :], w_in[base + j]).astype(BF16)
            buf[2 * j, local, :] = acc[:, :128]
            buf[2 * j + 1, local, :] = acc[:, 128:]
            return carry
        lax.fori_loop(0, per, step, 0)

    kv_local(per, k_buf)
    kv_local(2 * per, v_buf)

    to_right.wait()
    to_left.wait()
    normalise(0, BLOCK)
    normalise(BLOCK, BLOCK)
    normalise(LEFT + frames, BLOCK)

    def kv_halo(base, buf):
        def step(j, carry):
            rows = jnp.concatenate(
                [normed[pl.ds(0, LEFT), :], normed[pl.ds(LEFT + frames, BLOCK), :]], axis=0)
            acc = dot(rows, w_in[base + j]).astype(BF16)
            for side in range(2):
                part = acc[:, 128 * side : 128 * side + 128]
                buf[2 * j + side, pl.ds(0, LEFT), :] = part[:LEFT]
                buf[2 * j + side, pl.ds(LEFT + frames, BLOCK), :] = part[LEFT:]
            return carry
        lax.fori_loop(0, per, step, 0)

    kv_halo(per, k_buf)
    kv_halo(2 * per, v_buf)

    span = 256
    lane = lax.broadcasted_iota(jnp.int32, (2 * PAIR, 128), 1)
    q_row = lax.broadcasted_iota(jnp.int32, (2 * PAIR, 128), 0)
    later = (q_row // BLOCK) % 2
    indicator = jnp.where(lane == later, 1.0, 0.0).astype(BF16)
    low_half = lax.broadcasted_iota(jnp.int32, (PAIR, 128), 1) < 64
    ones = jnp.ones((span, 128), BF16)
    key_at = lax.broadcasted_iota(jnp.int32, (span, 128), 0)
    class_at = lax.broadcasted_iota(jnp.int32, (span, 128), 1)
    window = (key_at >= class_at * BLOCK) & (key_at < class_at * BLOCK + 4 * BLOCK)

    def attend(i, first):
        p = lax.rem(first + i, pairs)
        start = pl.multiple_of(p * PAIR, PAIR)
        key_frame = tm * frames + p * PAIR - LEFT + key_at
        usable = window & (key_frame >= 0) & (key_frame < total_frames)
        bias = jnp.where(usable | (class_at > 1), 0.0, MASKED).astype(BF16)
        for g in range(groups):
            q = q_buf[g, pl.ds(start, PAIR), :]
            zero = jnp.zeros_like(q)
            q = jnp.concatenate([jnp.where(low_half, q, zero), jnp.where(low_half, zero, q)], axis=0)
            q = jnp.concatenate([q, indicator], axis=1)
            k = jnp.concatenate([k_buf[g, pl.ds(start, span), :], bias], axis=1)
            scores = nt_dot(q, k)
            raised = jnp.exp2(scores - jnp.max(scores, axis=1, keepdims=True)).astype(BF16)
            v = jnp.concatenate([v_buf[g, pl.ds(start, span), :], ones], axis=1)
            result = dot(raised, v)
            numer = jnp.where(low_half, result[:PAIR, :128], result[PAIR:, :128])
            denom = jnp.where(low_half, result[:PAIR, 128:], result[PAIR:, 128:])
            att[pl.ds(start, PAIR), pl.ds(128 * g, 128)] = (numer / denom).astype(BF16)
        return first

    gate_row = mod[2:3, :]

    def project(starts, rows):
        def rows_of(ref, offset=0):
            return jnp.concatenate([ref[pl.ds(s + offset, rows), :] for s in starts], axis=0)
        for c in range(width // 256):
            cols = pl.ds(256 * c, 256)
            mixed = dot(rows_of(att), w_out[:, cols])
            held = jnp.concatenate(
                [hid[pl.ds(LEFT + s, rows), cols] for s in starts], axis=0).astype(F32)
            upd[:, cols] = (held + gate_row[:, 256 * c : 256 * c + 256] * mixed).astype(BF16)
        result = dot(upd[...], w_voc[...]).astype(BF16)
        for at, s in enumerate(starts):
            own[pl.ds(s, rows), :] = result[at * rows : (at + 1) * rows]

    quarter = frames // 4
    lax.fori_loop(0, pairs // 2, attend, 3 * pairs // 4)
    wout_copy.wait()
    wvoc_copy.wait()
    project((3 * quarter, 0), quarter)
    last, first = pl.ds(frames - RIM, RIM), pl.ds(0, RIM)
    before, after = pl.ds(lanes - RIM, RIM), pl.ds(frames, RIM)
    sent = [
        send(2, own.at[last], own.at[before], right),
        send(3, own.at[last], par.at[before], right_partner),
        send(4, own.at[first], own.at[after], left),
        send(5, own.at[first], par.at[after], left_partner),
    ]
    for i, s in ((6, 3 * quarter), (7, 0)):
        sent.append(send(i, own.at[pl.ds(s, quarter)], par.at[pl.ds(s, quarter)], partner))
    lax.fori_loop(0, pairs // 2, attend, pairs // 4)
    project((quarter,), 2 * quarter)
    middle = pl.ds(quarter, 2 * quarter)
    sent.append(send(8, own.at[middle], par.at[middle], partner))

    taps_copy.wait()
    alpha_copy.wait()
    pick_row = lax.broadcasted_iota(jnp.int32, (half, 2 * half), 0)
    pick_col = lax.broadcasted_iota(jnp.int32, (half, 2 * half), 1)
    picked = pick_col == pick_row + parity * half
    for k in range(4):
        taps_t[pl.ds(k * half, half), :] = taps[k, pl.ds(pl.multiple_of(parity * half, half), half), :]
    rate = jnp.sum(jnp.where(picked, alpha[...], 0.0), axis=1, keepdims=True)

    for copy in sent:
        copy.wait()

    own_is_cond = branch_ids[member] == 0
    strength = guidance[member // 2]
    own_weight = jnp.where(own_is_cond, strength, 1.0 - strength)
    par_weight = jnp.where(own_is_cond, 1.0 - strength, strength)
    frame_row = lax.broadcasted_iota(jnp.int32, (lanes, 1), 0)
    frame_row = jnp.where(frame_row < frames + 2 * RIM, frame_row, frame_row - lanes) + tm * frames
    inside = (frame_row >= 0) & (frame_row < total_frames)
    mixed = own_weight * own[...].astype(F32) + par_weight * par[...].astype(F32)
    guided[...] = jnp.where(inside, mixed, 0.0).astype(BF16)

    y_buf[...] = nt_dot(taps_t[...], guided[...])

    frame_lane = lax.broadcasted_iota(jnp.int32, (8, lanes), 1)
    frame_lane = jnp.where(frame_lane < frames + 2 * RIM, frame_lane, frame_lane - lanes) + tm * frames
    kept = (frame_lane >= 0) & (frame_lane < total_frames)

    def ahead(x, count):
        return pltpu.roll(x, (-count) % lanes, 1)

    for c in range(half // 8):
        rate_c = rate[8 * c : 8 * c + 8]
        turn = rate_c * (1.0 / math.pi)
        inverse = 1.0 / rate_c

        def snake(z):
            t = turn * z
            f = t - jnp.round(t)
            u = f * f
            s = SIN2[5]
            for a in (4, 3, 2, 1, 0):
                s = s * u + SIN2[a]
            return z + (s * u) * inverse

        y = [y_buf[pl.ds(k * half + 8 * c, 8), :] for k in range(4)]
        even = jnp.where(kept, y[1] + ahead(y[3], -1), 0.0)
        odd = jnp.where(kept, ahead(y[0], 1) + y[2], 0.0)
        even_p, odd_m = ahead(even, 1), ahead(odd, -1)
        b0, b1, b2, b3, b4, b5 = HALF_BAND
        between_even = (b0 * ahead(even, -1) + b1 * odd_m + b2 * even + b3 * odd
                        + b4 * even_p + b5 * ahead(odd, 1))
        between_odd = (b0 * odd_m + b1 * even + b2 * odd + b3 * even_p
                       + b4 * ahead(odd, 1) + b5 * ahead(even, 2))
        s_even = jnp.where(kept, snake(between_even), 0.0)
        s_odd = jnp.where(kept, snake(between_odd), 0.0)
        l0, l1, l2, l3, l4, l5 = LOW_PASS
        s_even_m, s_odd_m = ahead(s_even, -1), ahead(s_odd, -1)
        s_even_p, s_odd_p = ahead(s_even, 1), ahead(s_odd, 1)
        w_even = (CENTER_TAP * snake(even) + l0 * ahead(s_odd, -2) + l1 * s_even_m + l2 * s_odd_m
                  + l3 * s_even + l4 * s_odd + l5 * s_even_p)
        w_odd = (CENTER_TAP * snake(odd) + l0 * s_even_m + l1 * s_odd_m + l2 * s_even
                 + l3 * s_odd + l4 * s_even_p + l5 * s_odd_p)
        for b in range(frames // 128):
            wave[pl.ds(8 * c, 8), pl.ds(256 * b, 128)] = w_even[:, 128 * b : 128 * b + 128]
            wave[pl.ds(8 * c, 8), pl.ds(256 * b + 128, 128)] = w_odd[:, 128 * b : 128 * b + 128]

    for b in range(frames // 128):
        cols = pl.ds(256 * b, 256)
        out[:, cols] = dot(wave[:, cols].astype(BF16), perm[...]).astype(BF16)


def on_device(hidden_rows, modulation, project_in, project_out, to_vocoder, upsample_taps,
              snake_alpha, guidance, branch_ids):
    n_tm = lax.axis_size("tm")
    _, frames, width = hidden_rows.shape
    cin, cout = upsample_taps.shape[1:]
    half = cout // 2
    extent = LEFT + frames + BLOCK
    held = (frames // PAIR - 1) * PAIR + 256
    groups = width // 128
    lanes = -(-(frames + 2 * RIM) // 128) * 128
    any_spec = pl.BlockSpec(memory_space=pl.ANY)
    smem = pl.BlockSpec(memory_space=pltpu.SMEM)
    return pl.pallas_call(
        functools.partial(kernel, n_tm),
        out_shape=jax.ShapeDtypeStruct((half, 2 * frames), BF16),
        in_specs=[any_spec] * 7 + [smem] * 2,
        out_specs=pl.BlockSpec(memory_space=pltpu.VMEM),
        scratch_shapes=[
            pltpu.VMEM((extent, width), BF16),
            pltpu.VMEM((extent, width), BF16),
            pltpu.VMEM((3 * width // 256, width, 256), BF16),
            pltpu.VMEM((width, width), BF16),
            pltpu.VMEM((width, cin), BF16),
            pltpu.VMEM((4, cout, cin), BF16),
            pltpu.VMEM((3, width), F32),
            pltpu.VMEM((1, cout), F32),
            pltpu.VMEM((groups, frames, 128), BF16),
            pltpu.VMEM((groups, held, 128), BF16),
            pltpu.VMEM((groups, held, 128), BF16),
            pltpu.VMEM((frames, width), BF16),
            pltpu.VMEM((frames // 2, width), BF16),
            pltpu.VMEM((lanes, cin), BF16),
            pltpu.VMEM((lanes, cin), BF16),
            pltpu.VMEM((lanes, cin), BF16),
            pltpu.VMEM((4 * half, lanes), F32),
            pltpu.VMEM((half, 2 * frames), F32),
            pltpu.VMEM((4 * half, cin), BF16),
            pltpu.VMEM((256, 256), BF16),
            pltpu.SemaphoreType.DMA((3 * width // 256,)),
            pltpu.SemaphoreType.DMA((6,)),
            pltpu.SemaphoreType.DMA((9,)),
            pltpu.SemaphoreType.DMA((9,)),
        ],
        compiler_params=pltpu.CompilerParams(
            collective_id=0, has_side_effects=True, vmem_limit_bytes=56 * 1024 * 1024),
        cost_estimate=pl.CostEstimate(
            flops=9_000_000_000, bytes_accessed=12_000_000, transcendentals=3_000_000),
    )(hidden_rows, modulation.transpose(1, 0, 2), project_in, project_out, to_vocoder,
      upsample_taps.transpose(0, 2, 1), snake_alpha[None, :], guidance, branch_ids)


def solution(mesh):
    in_specs = (P("guide", "tm", None), P("guide", None, None), P(), P(), P(), P(), P(), P(), P())
    return jax.shard_map(
        on_device, mesh=mesh, in_specs=in_specs, out_specs=P("guide", "tm"), check_vma=False)
```

```python
import functools
import math

import jax
import jax.numpy as jnp
from jax import lax
from jax.experimental import pallas as pl
from jax.experimental.pallas import tpu as pltpu
from jax.sharding import PartitionSpec as P

HEADS = 16
BLOCK = 48
HALF_BAND = (3.0 / 256.0, -25.0 / 256.0, 150.0 / 256.0, 150.0 / 256.0, -25.0 / 256.0, 3.0 / 256.0)
LOW_PASS = (0.012, -0.06, 0.3, 0.3, -0.06, 0.012)
CENTER_TAP = 0.5
SIN2 = (9.869604202977849, -32.469663586217976, 42.72706432039706,
        -30.100639734504547, 13.048356860034854, -3.3563323291898937)
MASKED = -1e30
MESH = pl.DeviceIdType.MESH
F32 = jnp.float32
BF16 = jnp.bfloat16

PAIR = 2 * BLOCK
LEFT = 2 * BLOCK
RIM = 16


def nt_dot(a, b):
    return lax.dot_general(a, b, (((1,), (1,)), ((), ())), preferred_element_type=F32)


def dot(a, b):
    return jnp.dot(a, b, preferred_element_type=F32)


def kernel(n_tm, hidden, modulation, w_in_hbm, w_out_hbm, w_voc_hbm, taps_hbm, alpha_hbm,
           guidance, branch_ids, out,
           hid, normed, w_in, w_out, w_voc, taps, mod, alpha,
           q_buf, k_buf, v_buf, att, upd, own, par, guided, y_buf, wave, taps_t, perm,
           hid_sem, win_sem, in_sem, send_sem, recv_sem):
    frames = hidden.shape[1]
    width = hidden.shape[2]
    pairs = frames // PAIR
    groups = width // 128
    extent = LEFT + frames + BLOCK
    half = out.shape[0]
    lanes = own.shape[0]
    cin = own.shape[1]
    total_frames = n_tm * frames

    tm = lax.axis_index("tm")
    member = lax.axis_index("guide")
    parity = lax.rem(member, 2)
    other = member + 1 - 2 * parity
    right_tm = lax.rem(tm + 1, n_tm)
    left_tm = lax.rem(tm + n_tm - 1, n_tm)
    left, right = (left_tm, member), (right_tm, member)
    partner = (tm, other)
    left_partner, right_partner = (left_tm, other), (right_tm, other)

    def load(src, dst, sem):
        copy = pltpu.make_async_copy(src, dst, sem)
        copy.start()
        return copy

    parts = 4
    part = frames // parts
    hid_copies = [load(hidden.at[0, pl.ds(part * i, part)], hid.at[pl.ds(LEFT + part * i, part)],
                       hid_sem.at[i]) for i in range(parts)]
    mod_copy = load(modulation.at[:, 0], mod, in_sem.at[0])

    barrier = pltpu.get_barrier_semaphore()
    for device in (left, right, partner, left_partner, right_partner):
        pl.semaphore_signal(barrier, inc=1, device_id=device, device_id_type=MESH)

    def send(i, src, dst, device):
        copy = pltpu.make_async_remote_copy(
            src_ref=src, dst_ref=dst, send_sem=send_sem.at[i], recv_sem=recv_sem.at[i],
            device_id=device, device_id_type=MESH)
        copy.start()
        return copy

    def load_weights():
        tiles = w_in.shape[0]
        copies = [load(w_in_hbm.at[:, pl.ds(256 * j, 256)], w_in.at[j], win_sem.at[j])
                  for j in range(tiles)]
        for i, (src, dst) in enumerate(((w_out_hbm, w_out), (w_voc_hbm, w_voc),
                                        (taps_hbm, taps), (alpha_hbm, alpha))):
            copies.append(load(src, dst, in_sem.at[i + 1]))
        return copies[tiles:]

    hid_copies[0].wait()
    wout_copy, wvoc_copy, taps_copy, alpha_copy = load_weights()
    pl.semaphore_wait(barrier, 5)
    to_right = send(0, hidden.at[0, pl.ds(frames - LEFT, LEFT)], hid.at[pl.ds(0, LEFT)], right)
    to_left = send(1, hidden.at[0, pl.ds(0, BLOCK)], hid.at[pl.ds(LEFT + frames, BLOCK)], left)

    spare = k_buf.shape[1] - extent
    k_buf[:, pl.ds(extent, spare), :] = jnp.zeros((groups, spare, 128), BF16)
    v_buf[:, pl.ds(extent, spare), :] = jnp.zeros((groups, spare, 128), BF16)
    gap = lanes - frames - 2 * RIM
    own[pl.ds(frames + RIM, gap), :] = jnp.zeros((gap, cin), BF16)
    par[pl.ds(frames + RIM, gap), :] = jnp.zeros((gap, cin), BF16)
    row = lax.broadcasted_iota(jnp.int32, (256, 256), 0)
    col = lax.broadcasted_iota(jnp.int32, (256, 256), 1)
    perm[...] = jnp.where(row == (col % 2) * 128 + col // 2, 1.0, 0.0).astype(BF16)

    mod_copy.wait()
    scale_row = 1.0 + mod[0:1, :]
    shift_row = mod[1:2, :]

    def normalise(start, rows):
        x = hid[pl.ds(start, rows), :].astype(F32)
        centered = x - jnp.mean(x, axis=-1, keepdims=True)
        variance = jnp.mean(centered * centered, axis=-1, keepdims=True)
        result = centered * lax.rsqrt(variance + 1e-6) * scale_row + shift_row
        normed[pl.ds(start, rows), :] = result.astype(BF16)

    for i in range(parts):
        if i > 0:
            hid_copies[i].wait()

        def norm_step(j, carry):
            normalise(pl.multiple_of(LEFT + i * part + j * PAIR, PAIR), PAIR)
            return carry

        lax.fori_loop(0, part // PAIR, norm_step, 0)

    per = groups // 2
    local = pl.ds(LEFT, frames)

    def q_step(j, carry):
        pltpu.make_async_copy(w_in.at[j], w_in.at[j], win_sem.at[j]).wait()
        acc = dot(normed[local, :], w_in[j]) * (math.log2(math.e) / math.sqrt(width // HEADS))
        acc = acc.astype(BF16)
        q_buf[2 * j] = acc[:, :128]
        q_buf[2 * j + 1] = acc[:, 128:]
        return carry

    lax.fori_loop(0, per, q_step, 0)

    def keys_values(base, buf):
        def step(j, carry):
            pltpu.make_async_copy(w_in.at[base + j], w_in.at[base + j], win_sem.at[base + j]).wait()
            acc = dot(normed[...], w_in[base + j]).astype(BF16)
            buf[2 * j, pl.ds(0, extent), :] = acc[:, :128]
            buf[2 * j + 1, pl.ds(0, extent), :] = acc[:, 128:]
            return carry
        lax.fori_loop(0, per, step, 0)

    to_right.wait()
    to_left.wait()
    normalise(0, LEFT)
    normalise(LEFT + frames, BLOCK)
    keys_values(per, k_buf)
    keys_values(2 * per, v_buf)

    span = 256
    low_half = lax.broadcasted_iota(jnp.int32, (PAIR, 128), 1) < 64
    ones = jnp.ones((span, 128), BF16)
    key_at = lax.broadcasted_iota(jnp.int32, (PAIR, span), 1)
    block_at = lax.broadcasted_iota(jnp.int32, (PAIR, span), 0) // BLOCK * BLOCK
    window = (key_at >= block_at) & (key_at < block_at + 4 * BLOCK)

    def bias_of(p):
        usable = window
        if p == 0:
            usable = usable & ((key_at >= LEFT) | (tm > 0))
        if p == pairs - 1:
            usable = usable & ((key_at < LEFT + PAIR) | (tm < n_tm - 1))
        return jnp.where(usable, 0.0, MASKED)

    def attend(members):
        biases = {p: bias_of(p) for p in members}
        steps = [(p, g) for p in members for g in range(groups)]
        scores, raised = {}, {}

        def score(step):
            p, g = step
            q = q_buf[g, pl.ds(p * PAIR, PAIR), :]
            zero = jnp.zeros_like(q)
            q = jnp.concatenate([jnp.where(low_half, q, zero), jnp.where(low_half, zero, q)], axis=0)
            s = dot(q, jnp.transpose(k_buf[g, pl.ds(p * PAIR, span), :]))
            return jnp.concatenate([s[:PAIR] + biases[p], s[PAIR:] + biases[p]], axis=0)

        def raise_to(s):
            return jnp.exp2(s - jnp.max(s, axis=1, keepdims=True)).astype(BF16)

        def combine(step, weights):
            p, g = step
            v = jnp.concatenate([v_buf[g, pl.ds(p * PAIR, span), :], ones], axis=1)
            result = dot(weights, v)
            numer = jnp.where(low_half, result[:PAIR, :128], result[PAIR:, :128])
            denom = jnp.where(low_half, result[:PAIR, 128:], result[PAIR:, 128:])
            att[pl.ds(p * PAIR, PAIR), pl.ds(128 * g, 128)] = (numer / denom).astype(BF16)

        for t in range(len(steps) + 2):
            if t < len(steps):
                scores[t] = score(steps[t])
            if 0 <= t - 1 < len(steps):
                raised[t - 1] = raise_to(scores.pop(t - 1))
            if t >= 2:
                combine(steps[t - 2], raised.pop(t - 2))

    gate_row = mod[2:3, :]

    def project(starts, rows):
        def rows_of(ref, offset=0):
            return jnp.concatenate([ref[pl.ds(s + offset, rows), :] for s in starts], axis=0)
        for c in range(width // 256):
            cols = pl.ds(256 * c, 256)
            mixed = dot(rows_of(att), w_out[:, cols])
            held = jnp.concatenate(
                [hid[pl.ds(LEFT + s, rows), cols] for s in starts], axis=0).astype(F32)
            upd[:, cols] = (held + gate_row[:, 256 * c : 256 * c + 256] * mixed).astype(BF16)
        result = dot(upd[...], w_voc[...]).astype(BF16)
        for at, s in enumerate(starts):
            own[pl.ds(s, rows), :] = result[at * rows : (at + 1) * rows]

    quarter = frames // 4
    attend([(3 * pairs // 4 + i) % pairs for i in range(pairs // 2)])
    wout_copy.wait()
    wvoc_copy.wait()
    project((3 * quarter, 0), quarter)
    last, first = pl.ds(frames - RIM, RIM), pl.ds(0, RIM)
    before, after = pl.ds(lanes - RIM, RIM), pl.ds(frames, RIM)
    sent = [
        send(2, own.at[last], own.at[before], right),
        send(3, own.at[last], par.at[before], right_partner),
        send(4, own.at[first], own.at[after], left),
        send(5, own.at[first], par.at[after], left_partner),
    ]
    for i, s in ((6, 3 * quarter), (7, 0)):
        sent.append(send(i, own.at[pl.ds(s, quarter)], par.at[pl.ds(s, quarter)], partner))
    attend([pairs // 4 + i for i in range(pairs // 2)])
    project((quarter,), 2 * quarter)
    middle = pl.ds(quarter, 2 * quarter)
    sent.append(send(8, own.at[middle], par.at[middle], partner))

    taps_copy.wait()
    alpha_copy.wait()
    pick_row = lax.broadcasted_iota(jnp.int32, (half, 2 * half), 0)
    pick_col = lax.broadcasted_iota(jnp.int32, (half, 2 * half), 1)
    picked = pick_col == pick_row + parity * half
    for k in range(4):
        taps_t[pl.ds(k * half, half), :] = taps[k, pl.ds(pl.multiple_of(parity * half, half), half), :]
    rate = jnp.sum(jnp.where(picked, alpha[...], 0.0), axis=1, keepdims=True)

    for copy in sent:
        copy.wait()

    own_is_cond = branch_ids[member] == 0
    strength = guidance[member // 2]
    own_weight = jnp.where(own_is_cond, strength, 1.0 - strength)
    par_weight = jnp.where(own_is_cond, 1.0 - strength, strength)
    frame_row = lax.broadcasted_iota(jnp.int32, (lanes, 1), 0)
    frame_row = jnp.where(frame_row < frames + 2 * RIM, frame_row, frame_row - lanes) + tm * frames
    inside = (frame_row >= 0) & (frame_row < total_frames)
    mixed = own_weight * own[...].astype(F32) + par_weight * par[...].astype(F32)
    guided[...] = jnp.where(inside, mixed, 0.0).astype(BF16)

    y_buf[...] = nt_dot(taps_t[...], guided[...])

    frame_lane = lax.broadcasted_iota(jnp.int32, (8, lanes), 1)
    frame_lane = jnp.where(frame_lane < frames + 2 * RIM, frame_lane, frame_lane - lanes) + tm * frames
    kept = (frame_lane >= 0) & (frame_lane < total_frames)

    def ahead(x, count):
        return pltpu.roll(x, (-count) % lanes, 1)

    for c in range(half // 8):
        rate_c = rate[8 * c : 8 * c + 8]
        turn = rate_c * (1.0 / math.pi)
        inverse = 1.0 / rate_c

        def snake(z):
            t = turn * z
            f = t - jnp.round(t)
            u = f * f
            s = SIN2[5]
            for a in (4, 3, 2, 1, 0):
                s = s * u + SIN2[a]
            return z + (s * u) * inverse

        y = [y_buf[pl.ds(k * half + 8 * c, 8), :] for k in range(4)]
        even = jnp.where(kept, y[1] + ahead(y[3], -1), 0.0)
        odd = jnp.where(kept, ahead(y[0], 1) + y[2], 0.0)
        even_p, odd_m = ahead(even, 1), ahead(odd, -1)
        b0, b1, b2, b3, b4, b5 = HALF_BAND
        between_even = (b0 * ahead(even, -1) + b1 * odd_m + b2 * even + b3 * odd
                        + b4 * even_p + b5 * ahead(odd, 1))
        between_odd = (b0 * odd_m + b1 * even + b2 * odd + b3 * even_p
                       + b4 * ahead(odd, 1) + b5 * ahead(even, 2))
        s_even = jnp.where(kept, snake(between_even), 0.0)
        s_odd = jnp.where(kept, snake(between_odd), 0.0)
        l0, l1, l2, l3, l4, l5 = LOW_PASS
        s_even_m, s_odd_m = ahead(s_even, -1), ahead(s_odd, -1)
        s_even_p, s_odd_p = ahead(s_even, 1), ahead(s_odd, 1)
        w_even = (CENTER_TAP * snake(even) + l0 * ahead(s_odd, -2) + l1 * s_even_m + l2 * s_odd_m
                  + l3 * s_even + l4 * s_odd + l5 * s_even_p)
        w_odd = (CENTER_TAP * snake(odd) + l0 * s_even_m + l1 * s_odd_m + l2 * s_even
                 + l3 * s_odd + l4 * s_even_p + l5 * s_odd_p)
        for b in range(frames // 128):
            wave[pl.ds(8 * c, 8), pl.ds(256 * b, 128)] = w_even[:, 128 * b : 128 * b + 128]
            wave[pl.ds(8 * c, 8), pl.ds(256 * b + 128, 128)] = w_odd[:, 128 * b : 128 * b + 128]

    for b in range(frames // 128):
        cols = pl.ds(256 * b, 256)
        out[:, cols] = dot(wave[:, cols].astype(BF16), perm[...]).astype(BF16)


def on_device(hidden_rows, modulation, project_in, project_out, to_vocoder, upsample_taps,
              snake_alpha, guidance, branch_ids):
    n_tm = lax.axis_size("tm")
    _, frames, width = hidden_rows.shape
    cin, cout = upsample_taps.shape[1:]
    half = cout // 2
    extent = LEFT + frames + BLOCK
    held = (frames // PAIR - 1) * PAIR + 256
    groups = width // 128
    lanes = -(-(frames + 2 * RIM) // 128) * 128
    any_spec = pl.BlockSpec(memory_space=pl.ANY)
    smem = pl.BlockSpec(memory_space=pltpu.SMEM)
    return pl.pallas_call(
        functools.partial(kernel, n_tm),
        out_shape=jax.ShapeDtypeStruct((half, 2 * frames), BF16),
        in_specs=[any_spec] * 7 + [smem] * 2,
        out_specs=pl.BlockSpec(memory_space=pltpu.VMEM),
        scratch_shapes=[
            pltpu.VMEM((extent, width), BF16),
            pltpu.VMEM((extent, width), BF16),
            pltpu.VMEM((3 * width // 256, width, 256), BF16),
            pltpu.VMEM((width, width), BF16),
            pltpu.VMEM((width, cin), BF16),
            pltpu.VMEM((4, cout, cin), BF16),
            pltpu.VMEM((3, width), F32),
            pltpu.VMEM((1, cout), F32),
            pltpu.VMEM((groups, frames, 128), BF16),
            pltpu.VMEM((groups, held, 128), BF16),
            pltpu.VMEM((groups, held, 128), BF16),
            pltpu.VMEM((frames, width), BF16),
            pltpu.VMEM((frames // 2, width), BF16),
            pltpu.VMEM((lanes, cin), BF16),
            pltpu.VMEM((lanes, cin), BF16),
            pltpu.VMEM((lanes, cin), BF16),
            pltpu.VMEM((4 * half, lanes), F32),
            pltpu.VMEM((half, 2 * frames), F32),
            pltpu.VMEM((4 * half, cin), BF16),
            pltpu.VMEM((256, 256), BF16),
            pltpu.SemaphoreType.DMA((4,)),
            pltpu.SemaphoreType.DMA((3 * width // 256,)),
            pltpu.SemaphoreType.DMA((5,)),
            pltpu.SemaphoreType.DMA((9,)),
            pltpu.SemaphoreType.DMA((9,)),
        ],
        compiler_params=pltpu.CompilerParams(
            collective_id=0, has_side_effects=True, vmem_limit_bytes=56 * 1024 * 1024),
        cost_estimate=pl.CostEstimate(
            flops=9_000_000_000, bytes_accessed=12_000_000, transcendentals=3_000_000),
    )(hidden_rows, modulation.transpose(1, 0, 2), project_in, project_out, to_vocoder,
      upsample_taps.transpose(0, 2, 1), snake_alpha[None, :], guidance, branch_ids)


def solution(mesh):
    in_specs = (P("guide", "tm", None), P("guide", None, None), P(), P(), P(), P(), P(), P(), P())
    return jax.shard_map(
        on_device, mesh=mesh, in_specs=in_specs, out_specs=P("guide", "tm"), check_vma=False)
```

```python
import functools
import math

import jax
import jax.numpy as jnp
from jax import lax
from jax.experimental import pallas as pl
from jax.experimental.pallas import tpu as pltpu
from jax.sharding import PartitionSpec as P

HEADS = 16
BLOCK = 48
HALF_BAND = (3.0 / 256.0, -25.0 / 256.0, 150.0 / 256.0, 150.0 / 256.0, -25.0 / 256.0, 3.0 / 256.0)
LOW_PASS = (0.012, -0.06, 0.3, 0.3, -0.06, 0.012)
CENTER_TAP = 0.5
SIN2 = (9.869604202977849, -32.469663586217976, 42.72706432039706,
        -30.100639734504547, 13.048356860034854, -3.3563323291898937)
MASKED = -1e30
MESH = pl.DeviceIdType.MESH
F32 = jnp.float32
BF16 = jnp.bfloat16

PAIR = 2 * BLOCK
LEFT = 2 * BLOCK
RIM = 16


def nt_dot(a, b):
    return lax.dot_general(a, b, (((1,), (1,)), ((), ())), preferred_element_type=F32)


def dot(a, b):
    return jnp.dot(a, b, preferred_element_type=F32)


def kernel(n_tm, hidden, modulation, w_in_hbm, w_out_hbm, w_voc_hbm, taps_hbm, alpha_hbm,
           guidance, branch_ids, out,
           hid, normed, w_in, w_out, w_voc, taps, mod, alpha,
           q_buf, k_buf, v_buf, att, upd, own, par, guided, y_buf, wave, taps_t, perm,
           hid_sem, win_sem, in_sem, send_sem, recv_sem):
    frames = hidden.shape[1]
    width = hidden.shape[2]
    pairs = frames // PAIR
    groups = width // 128
    extent = LEFT + frames + BLOCK
    half = out.shape[0]
    lanes = own.shape[0]
    cin = own.shape[1]
    total_frames = n_tm * frames

    tm = lax.axis_index("tm")
    member = lax.axis_index("guide")
    parity = lax.rem(member, 2)
    other = member + 1 - 2 * parity
    has_left, has_right = tm > 0, tm < n_tm - 1
    late = tm == n_tm // 2
    prompt = jnp.logical_not(late)
    left_tm, right_tm = jnp.maximum(tm - 1, 0), jnp.minimum(tm + 1, n_tm - 1)
    left, right = (left_tm, member), (right_tm, member)
    partner = (tm, other)
    left_partner, right_partner = (left_tm, other), (right_tm, other)

    def load(src, dst, sem):
        copy = pltpu.make_async_copy(src, dst, sem)
        copy.start()
        return copy

    parts = 4
    part = frames // parts
    hid_copies = [load(hidden.at[0, pl.ds(part * i, part)], hid.at[pl.ds(LEFT + part * i, part)],
                       hid_sem.at[i]) for i in range(parts)]
    mod_copy = load(modulation.at[:, 0], mod, in_sem.at[0])

    barrier = pltpu.get_barrier_semaphore()

    def greet(*devices):
        for device in devices:
            pl.semaphore_signal(barrier, inc=1, device_id=device, device_id_type=MESH)

    greet(partner)
    pl.when(has_left)(lambda: greet(left, left_partner))
    pl.when(has_right)(lambda: greet(right, right_partner))

    def transfer(i, src, dst, device):
        return pltpu.make_async_remote_copy(
            src_ref=src, dst_ref=dst, send_sem=send_sem.at[i], recv_sem=recv_sem.at[i],
            device_id=device, device_id_type=MESH)

    def start(*copies):
        for copy in copies:
            copy.start()

    def wait(sent, received):
        for copy in sent:
            copy.wait_send()
        for copy in received:
            copy.wait_recv()

    def load_weights():
        tiles = w_in.shape[0]
        copies = [load(w_in_hbm.at[:, pl.ds(256 * j, 256)], w_in.at[j], win_sem.at[j])
                  for j in range(tiles)]
        for i, (src, dst) in enumerate(((w_out_hbm, w_out), (w_voc_hbm, w_voc),
                                        (taps_hbm, taps), (alpha_hbm, alpha))):
            copies.append(load(src, dst, in_sem.at[i + 1]))
        return copies[tiles:]

    hid_copies[0].wait()
    wout_copy, wvoc_copy, taps_copy, alpha_copy = load_weights()

    to_right = transfer(0, hidden.at[0, pl.ds(frames - LEFT, LEFT)], hid.at[pl.ds(0, LEFT)], right)
    to_left = transfer(1, hidden.at[0, pl.ds(0, BLOCK)], hid.at[pl.ds(LEFT + frames, BLOCK)], left)

    def share_hidden():
        pl.semaphore_wait(
            barrier, 1 + 2 * has_left.astype(jnp.int32) + 2 * has_right.astype(jnp.int32))
        pl.when(has_right)(lambda: start(to_right))
        pl.when(has_left)(lambda: start(to_left))

    spare = k_buf.shape[1] - extent
    k_buf[:, pl.ds(extent, spare), :] = jnp.zeros((groups, spare, 128), BF16)
    v_buf[:, pl.ds(extent, spare), :] = jnp.zeros((groups, spare, 128), BF16)
    gap = lanes - frames - 2 * RIM

    def clear(start, count):
        own[pl.ds(start, count), :] = jnp.zeros((count, cin), BF16)
        par[pl.ds(start, count), :] = jnp.zeros((count, cin), BF16)

    clear(frames + RIM, gap)

    @pl.when(tm == 0)
    def _():
        hid[pl.ds(0, LEFT), :] = jnp.zeros((LEFT, width), BF16)
        clear(lanes - RIM, RIM)

    @pl.when(tm == n_tm - 1)
    def _():
        hid[pl.ds(LEFT + frames, BLOCK), :] = jnp.zeros((BLOCK, width), BF16)
        clear(frames, RIM)

    row = lax.broadcasted_iota(jnp.int32, (256, 256), 0)
    col = lax.broadcasted_iota(jnp.int32, (256, 256), 1)
    perm[...] = jnp.where(row == (col % 2) * 128 + col // 2, 1.0, 0.0).astype(BF16)

    mod_copy.wait()
    scale_row = 1.0 + mod[0:1, :]
    shift_row = mod[1:2, :]

    def normalise(start, rows):
        x = hid[pl.ds(start, rows), :].astype(F32)
        centered = x - jnp.mean(x, axis=-1, keepdims=True)
        variance = jnp.mean(centered * centered, axis=-1, keepdims=True)
        result = centered * lax.rsqrt(variance + 1e-6) * scale_row + shift_row
        normed[pl.ds(start, rows), :] = result.astype(BF16)

    for i in range(parts):
        if i > 0:
            hid_copies[i].wait()

        def norm_step(j, carry):
            normalise(pl.multiple_of(LEFT + i * part + j * PAIR, PAIR), PAIR)
            return carry

        lax.fori_loop(0, part // PAIR, norm_step, 0)
        if i == 1:
            pl.when(prompt)(share_hidden)

    per = groups // 2
    local = pl.ds(LEFT, frames)

    def q_step(j, carry):
        pltpu.make_async_copy(w_in.at[j], w_in.at[j], win_sem.at[j]).wait()
        acc = dot(normed[local, :], w_in[j]) * (math.log2(math.e) / math.sqrt(width // HEADS))
        acc = acc.astype(BF16)
        q_buf[2 * j] = acc[:, :128]
        q_buf[2 * j + 1] = acc[:, 128:]
        return carry

    lax.fori_loop(0, per, q_step, 0)

    pl.when(late)(share_hidden)

    def keys_values(base, buf):
        def step(j, carry):
            pltpu.make_async_copy(w_in.at[base + j], w_in.at[base + j], win_sem.at[base + j]).wait()
            acc = dot(normed[local, :], w_in[base + j]).astype(BF16)
            buf[2 * j, local, :] = acc[:, :128]
            buf[2 * j + 1, local, :] = acc[:, 128:]
            return carry
        lax.fori_loop(0, per, step, 0)

    keys_values(per, k_buf)
    keys_values(2 * per, v_buf)

    span = 256
    low_half = lax.broadcasted_iota(jnp.int32, (PAIR, 128), 1) < 64
    ones = jnp.ones((span, 128), BF16)
    key_at = lax.broadcasted_iota(jnp.int32, (PAIR, span), 1)
    block_at = lax.broadcasted_iota(jnp.int32, (PAIR, span), 0) // BLOCK * BLOCK
    window = (key_at >= block_at) & (key_at < block_at + 4 * BLOCK)

    def bias_of(p):
        usable = window
        if p == 0:
            usable = usable & ((key_at >= LEFT) | (tm > 0))
        if p == pairs - 1:
            usable = usable & ((key_at < LEFT + PAIR) | (tm < n_tm - 1))
        return jnp.where(usable, 0.0, MASKED)

    def attend(members):
        biases = {p: bias_of(p) for p in members}
        steps = [(p, g) for p in members for g in range(groups)]
        scores, raised = {}, {}

        def score(step):
            p, g = step
            q = q_buf[g, pl.ds(p * PAIR, PAIR), :]
            zero = jnp.zeros_like(q)
            q = jnp.concatenate([jnp.where(low_half, q, zero), jnp.where(low_half, zero, q)], axis=0)
            s = dot(q, jnp.transpose(k_buf[g, pl.ds(p * PAIR, span), :]))
            return jnp.concatenate([s[:PAIR] + biases[p], s[PAIR:] + biases[p]], axis=0)

        def raise_to(s):
            return jnp.exp2(s - jnp.max(s, axis=1, keepdims=True)).astype(BF16)

        def combine(step, weights):
            p, g = step
            v = jnp.concatenate([v_buf[g, pl.ds(p * PAIR, span), :], ones], axis=1)
            result = dot(weights, v)
            numer = jnp.where(low_half, result[:PAIR, :128], result[PAIR:, :128])
            denom = jnp.where(low_half, result[:PAIR, 128:], result[PAIR:, 128:])
            att[pl.ds(p * PAIR, PAIR), pl.ds(128 * g, 128)] = (numer / denom).astype(BF16)

        for t in range(len(steps) + 2):
            if t < len(steps):
                scores[t] = score(steps[t])
            if 0 <= t - 1 < len(steps):
                raised[t - 1] = raise_to(scores.pop(t - 1))
            if t >= 2:
                combine(steps[t - 2], raised.pop(t - 2))

    gate_row = mod[2:3, :]

    def project(starts, rows):
        def rows_of(ref, offset=0):
            return jnp.concatenate([ref[pl.ds(s + offset, rows), :] for s in starts], axis=0)
        for c in range(width // 256):
            cols = pl.ds(256 * c, 256)
            mixed = dot(rows_of(att), w_out[:, cols])
            held = jnp.concatenate(
                [hid[pl.ds(LEFT + s, rows), cols] for s in starts], axis=0).astype(F32)
            upd[:, cols] = (held + gate_row[:, 256 * c : 256 * c + 256] * mixed).astype(BF16)
        result = dot(upd[...], w_voc[...]).astype(BF16)
        for at, s in enumerate(starts):
            own[pl.ds(s, rows), :] = result[at * rows : (at + 1) * rows]

    quarter = frames // 4
    last, first = pl.ds(frames - RIM, RIM), pl.ds(0, RIM)
    before, after = pl.ds(lanes - RIM, RIM), pl.ds(frames, RIM)
    rightward = (transfer(2, own.at[last], own.at[before], right),
                 transfer(3, own.at[last], par.at[before], right_partner))
    leftward = (transfer(4, own.at[first], own.at[after], left),
                transfer(5, own.at[first], par.at[after], left_partner))
    shared = [transfer(i, own.at[pl.ds(s, n)], par.at[pl.ds(s, n)], partner)
              for i, s, n in ((6, 3 * quarter, quarter), (7, 0, quarter), (8, quarter, 2 * quarter))]

    wout_copy.wait()
    wvoc_copy.wait()

    def inner_half():
        attend([pairs // 4 + i for i in range(pairs // 2)])
        project((quarter,), 2 * quarter)
        start(shared[2])

    pl.when(late)(inner_half)

    pl.when(has_left)(lambda: wait((to_left,), (to_right,)))
    pl.when(has_right)(lambda: wait((to_right,), (to_left,)))
    normalise(0, LEFT)
    normalise(LEFT + frames, BLOCK)
    rim_rows = jnp.concatenate(
        [normed[pl.ds(0, LEFT), :], normed[pl.ds(LEFT + frames, BLOCK), :]], axis=0)

    def rim_keys_values(base, buf):
        def step(j, carry):
            acc = dot(rim_rows, w_in[base + j]).astype(BF16)
            for side in range(2):
                part = acc[:, 128 * side : 128 * side + 128]
                buf[2 * j + side, pl.ds(0, LEFT), :] = part[:LEFT]
                buf[2 * j + side, pl.ds(LEFT + frames, BLOCK), :] = part[LEFT:]
            return carry
        lax.fori_loop(0, per, step, 0)

    rim_keys_values(per, k_buf)
    rim_keys_values(2 * per, v_buf)

    attend([(3 * pairs // 4 + i) % pairs for i in range(pairs // 2)])
    project((3 * quarter, 0), quarter)
    pl.when(has_right)(lambda: start(*rightward))
    pl.when(has_left)(lambda: start(*leftward))
    start(*shared[:2])

    pl.when(prompt)(inner_half)

    taps_copy.wait()
    alpha_copy.wait()
    pick_row = lax.broadcasted_iota(jnp.int32, (half, 2 * half), 0)
    pick_col = lax.broadcasted_iota(jnp.int32, (half, 2 * half), 1)
    picked = pick_col == pick_row + parity * half
    for k in range(4):
        taps_t[pl.ds(k * half, half), :] = taps[k, pl.ds(pl.multiple_of(parity * half, half), half), :]
    rate = jnp.sum(jnp.where(picked, alpha[...], 0.0), axis=1, keepdims=True)

    pl.when(has_right)(lambda: wait(rightward, leftward))
    pl.when(has_left)(lambda: wait(leftward, rightward))
    wait(shared, shared)

    own_is_cond = branch_ids[member] == 0
    strength = guidance[member // 2]
    own_weight = jnp.where(own_is_cond, strength, 1.0 - strength)
    par_weight = jnp.where(own_is_cond, 1.0 - strength, strength)
    frame_row = lax.broadcasted_iota(jnp.int32, (lanes, 1), 0)
    frame_row = jnp.where(frame_row < frames + 2 * RIM, frame_row, frame_row - lanes) + tm * frames
    inside = (frame_row >= 0) & (frame_row < total_frames)
    mixed = own_weight * own[...].astype(F32) + par_weight * par[...].astype(F32)
    guided[...] = jnp.where(inside, mixed, 0.0).astype(BF16)

    y_buf[...] = nt_dot(taps_t[...], guided[...])

    frame_lane = lax.broadcasted_iota(jnp.int32, (8, lanes), 1)
    frame_lane = jnp.where(frame_lane < frames + 2 * RIM, frame_lane, frame_lane - lanes) + tm * frames
    kept = (frame_lane >= 0) & (frame_lane < total_frames)

    def ahead(x, count):
        return pltpu.roll(x, (-count) % lanes, 1)

    for c in range(half // 8):
        rate_c = rate[8 * c : 8 * c + 8]
        turn = rate_c * (1.0 / math.pi)
        inverse = 1.0 / rate_c

        def snake(z):
            t = turn * z
            f = t - jnp.round(t)
            u = f * f
            s = SIN2[5]
            for a in (4, 3, 2, 1, 0):
                s = s * u + SIN2[a]
            return z + (s * u) * inverse

        y = [y_buf[pl.ds(k * half + 8 * c, 8), :] for k in range(4)]
        even = jnp.where(kept, y[1] + ahead(y[3], -1), 0.0)
        odd = jnp.where(kept, ahead(y[0], 1) + y[2], 0.0)
        even_p, odd_m = ahead(even, 1), ahead(odd, -1)
        b0, b1, b2, b3, b4, b5 = HALF_BAND
        between_even = (b0 * ahead(even, -1) + b1 * odd_m + b2 * even + b3 * odd
                        + b4 * even_p + b5 * ahead(odd, 1))
        between_odd = (b0 * odd_m + b1 * even + b2 * odd + b3 * even_p
                       + b4 * ahead(odd, 1) + b5 * ahead(even, 2))
        s_even = jnp.where(kept, snake(between_even), 0.0)
        s_odd = jnp.where(kept, snake(between_odd), 0.0)
        l0, l1, l2, l3, l4, l5 = LOW_PASS
        s_even_m, s_odd_m = ahead(s_even, -1), ahead(s_odd, -1)
        s_even_p, s_odd_p = ahead(s_even, 1), ahead(s_odd, 1)
        w_even = (CENTER_TAP * snake(even) + l0 * ahead(s_odd, -2) + l1 * s_even_m + l2 * s_odd_m
                  + l3 * s_even + l4 * s_odd + l5 * s_even_p)
        w_odd = (CENTER_TAP * snake(odd) + l0 * s_even_m + l1 * s_odd_m + l2 * s_even
                 + l3 * s_odd + l4 * s_even_p + l5 * s_odd_p)
        for b in range(frames // 128):
            wave[pl.ds(8 * c, 8), pl.ds(256 * b, 128)] = w_even[:, 128 * b : 128 * b + 128]
            wave[pl.ds(8 * c, 8), pl.ds(256 * b + 128, 128)] = w_odd[:, 128 * b : 128 * b + 128]

    for b in range(frames // 128):
        cols = pl.ds(256 * b, 256)
        out[:, cols] = dot(wave[:, cols].astype(BF16), perm[...]).astype(BF16)


def on_device(hidden_rows, modulation, project_in, project_out, to_vocoder, upsample_taps,
              snake_alpha, guidance, branch_ids):
    n_tm = lax.axis_size("tm")
    _, frames, width = hidden_rows.shape
    cin, cout = upsample_taps.shape[1:]
    half = cout // 2
    extent = LEFT + frames + BLOCK
    held = (frames // PAIR - 1) * PAIR + 256
    groups = width // 128
    lanes = -(-(frames + 2 * RIM) // 128) * 128
    any_spec = pl.BlockSpec(memory_space=pl.ANY)
    smem = pl.BlockSpec(memory_space=pltpu.SMEM)
    return pl.pallas_call(
        functools.partial(kernel, n_tm),
        out_shape=jax.ShapeDtypeStruct((half, 2 * frames), BF16),
        in_specs=[any_spec] * 7 + [smem] * 2,
        out_specs=pl.BlockSpec(memory_space=pltpu.VMEM),
        scratch_shapes=[
            pltpu.VMEM((extent, width), BF16),
            pltpu.VMEM((extent, width), BF16),
            pltpu.VMEM((3 * width // 256, width, 256), BF16),
            pltpu.VMEM((width, width), BF16),
            pltpu.VMEM((width, cin), BF16),
            pltpu.VMEM((4, cout, cin), BF16),
            pltpu.VMEM((3, width), F32),
            pltpu.VMEM((1, cout), F32),
            pltpu.VMEM((groups, frames, 128), BF16),
            pltpu.VMEM((groups, held, 128), BF16),
            pltpu.VMEM((groups, held, 128), BF16),
            pltpu.VMEM((frames, width), BF16),
            pltpu.VMEM((frames // 2, width), BF16),
            pltpu.VMEM((lanes, cin), BF16),
            pltpu.VMEM((lanes, cin), BF16),
            pltpu.VMEM((lanes, cin), BF16),
            pltpu.VMEM((4 * half, lanes), F32),
            pltpu.VMEM((half, 2 * frames), F32),
            pltpu.VMEM((4 * half, cin), BF16),
            pltpu.VMEM((256, 256), BF16),
            pltpu.SemaphoreType.DMA((4,)),
            pltpu.SemaphoreType.DMA((3 * width // 256,)),
            pltpu.SemaphoreType.DMA((5,)),
            pltpu.SemaphoreType.DMA((9,)),
            pltpu.SemaphoreType.DMA((9,)),
        ],
        compiler_params=pltpu.CompilerParams(
            collective_id=0, has_side_effects=True, vmem_limit_bytes=56 * 1024 * 1024),
        cost_estimate=pl.CostEstimate(
            flops=9_000_000_000, bytes_accessed=12_000_000, transcendentals=3_000_000),
    )(hidden_rows, modulation.transpose(1, 0, 2), project_in, project_out, to_vocoder,
      upsample_taps.transpose(0, 2, 1), snake_alpha[None, :], guidance, branch_ids)


def solution(mesh):
    in_specs = (P("guide", "tm", None), P("guide", None, None), P(), P(), P(), P(), P(), P(), P())
    return jax.shard_map(
        on_device, mesh=mesh, in_specs=in_specs, out_specs=P("guide", "tm"), check_vma=False)
```

```python
import functools
import math

import jax
import jax.numpy as jnp
from jax import lax
from jax.experimental import pallas as pl
from jax.experimental.pallas import tpu as pltpu
from jax.sharding import PartitionSpec as P

HEADS = 16
BLOCK = 48
HALF_BAND = (3.0 / 256.0, -25.0 / 256.0, 150.0 / 256.0, 150.0 / 256.0, -25.0 / 256.0, 3.0 / 256.0)
LOW_PASS = (0.012, -0.06, 0.3, 0.3, -0.06, 0.012)
CENTER_TAP = 0.5
SIN2 = (9.869604202977849, -32.469663586217976, 42.72706432039706,
        -30.100639734504547, 13.048356860034854, -3.3563323291898937)
MASKED = -1e30
MESH = pl.DeviceIdType.MESH
F32 = jnp.float32
BF16 = jnp.bfloat16

PAIR = 2 * BLOCK
LEFT = 2 * BLOCK
RIM = 16


def nt_dot(a, b):
    return lax.dot_general(a, b, (((1,), (1,)), ((), ())), preferred_element_type=F32)


def dot(a, b):
    return jnp.dot(a, b, preferred_element_type=F32)


def kernel(n_tm, hidden, modulation, w_in_hbm, w_out_hbm, w_voc_hbm, taps_hbm, alpha_hbm,
           guidance, branch_ids, out,
           hid, normed, w_in, w_out, w_voc, taps, mod, alpha,
           q_buf, k_buf, v_buf, att, upd, own, par, guided, y_buf, wave, taps_t, perm,
           hid_sem, win_sem, in_sem, send_sem, recv_sem):
    frames = hidden.shape[1]
    width = hidden.shape[2]
    pairs = frames // PAIR
    groups = width // 128
    extent = LEFT + frames + BLOCK
    half = out.shape[0]
    lanes = own.shape[0]
    cin = own.shape[1]
    total_frames = n_tm * frames

    tm = lax.axis_index("tm")
    member = lax.axis_index("guide")
    parity = lax.rem(member, 2)
    other = member + 1 - 2 * parity
    has_left, has_right = tm > 0, tm < n_tm - 1
    late = tm == n_tm // 2
    prompt = jnp.logical_not(late)
    left_tm, right_tm = jnp.maximum(tm - 1, 0), jnp.minimum(tm + 1, n_tm - 1)
    left, right = (left_tm, member), (right_tm, member)
    partner = (tm, other)
    left_partner, right_partner = (left_tm, other), (right_tm, other)

    def load(src, dst, sem):
        copy = pltpu.make_async_copy(src, dst, sem)
        copy.start()
        return copy

    parts = 4
    part = frames // parts
    hid_copies = [load(hidden.at[0, pl.ds(part * i, part)], hid.at[pl.ds(LEFT + part * i, part)],
                       hid_sem.at[i]) for i in range(parts)]
    mod_copy = load(modulation.at[:, 0], mod, in_sem.at[0])

    barrier = pltpu.get_barrier_semaphore()

    def greet(*devices):
        for device in devices:
            pl.semaphore_signal(barrier, inc=1, device_id=device, device_id_type=MESH)

    greet(partner)
    pl.when(has_left)(lambda: greet(left, left_partner))
    pl.when(has_right)(lambda: greet(right, right_partner))

    def transfer(i, src, dst, device):
        return pltpu.make_async_remote_copy(
            src_ref=src, dst_ref=dst, send_sem=send_sem.at[i], recv_sem=recv_sem.at[i],
            device_id=device, device_id_type=MESH)

    def start(*copies):
        for copy in copies:
            copy.start()

    def wait(sent, received):
        for copy in sent:
            copy.wait_send()
        for copy in received:
            copy.wait_recv()

    def load_weights():
        tiles = w_in.shape[0]
        copies = [load(w_in_hbm.at[:, pl.ds(256 * j, 256)], w_in.at[j], win_sem.at[j])
                  for j in range(tiles)]
        for i, (src, dst) in enumerate(((w_out_hbm, w_out), (w_voc_hbm, w_voc),
                                        (taps_hbm, taps), (alpha_hbm, alpha))):
            copies.append(load(src, dst, in_sem.at[i + 1]))
        return copies[tiles:]

    hid_copies[0].wait()
    wout_copy, wvoc_copy, taps_copy, alpha_copy = load_weights()

    to_right = transfer(0, hidden.at[0, pl.ds(frames - LEFT, LEFT)], hid.at[pl.ds(0, LEFT)], right)
    to_left = transfer(1, hidden.at[0, pl.ds(0, BLOCK)], hid.at[pl.ds(LEFT + frames, BLOCK)], left)

    def share_hidden():
        pl.semaphore_wait(
            barrier, 1 + 2 * has_left.astype(jnp.int32) + 2 * has_right.astype(jnp.int32))
        pl.when(has_right)(lambda: start(to_right))
        pl.when(has_left)(lambda: start(to_left))

    spare = k_buf.shape[1] - extent
    k_buf[:, pl.ds(extent, spare), :] = jnp.zeros((groups, spare, 128), BF16)
    v_buf[:, pl.ds(extent, spare), :] = jnp.zeros((groups, spare, 128), BF16)
    gap = lanes - frames - 2 * RIM

    def clear(start, count):
        own[pl.ds(start, count), :] = jnp.zeros((count, cin), BF16)
        par[pl.ds(start, count), :] = jnp.zeros((count, cin), BF16)

    clear(frames + RIM, gap)

    @pl.when(tm == 0)
    def _():
        hid[pl.ds(0, LEFT), :] = jnp.zeros((LEFT, width), BF16)
        clear(lanes - RIM, RIM)

    @pl.when(tm == n_tm - 1)
    def _():
        hid[pl.ds(LEFT + frames, BLOCK), :] = jnp.zeros((BLOCK, width), BF16)
        clear(frames, RIM)

    row = lax.broadcasted_iota(jnp.int32, (256, 256), 0)
    col = lax.broadcasted_iota(jnp.int32, (256, 256), 1)
    perm[...] = jnp.where(row == (col % 2) * 128 + col // 2, 1.0, 0.0).astype(BF16)

    mod_copy.wait()
    scale_row = 1.0 + mod[0:1, :]
    shift_row = mod[1:2, :]

    def normalise(start, rows):
        x = hid[pl.ds(start, rows), :].astype(F32)
        centered = x - jnp.mean(x, axis=-1, keepdims=True)
        variance = jnp.mean(centered * centered, axis=-1, keepdims=True)
        result = centered * lax.rsqrt(variance + 1e-6) * scale_row + shift_row
        normed[pl.ds(start, rows), :] = result.astype(BF16)

    for i in range(parts):
        if i > 0:
            hid_copies[i].wait()

        def norm_step(j, carry):
            normalise(pl.multiple_of(LEFT + i * part + j * PAIR, PAIR), PAIR)
            return carry

        lax.fori_loop(0, part // PAIR, norm_step, 0)
        if i == 1:
            pl.when(prompt)(share_hidden)

    per = groups // 2
    local = pl.ds(LEFT, frames)

    def arrived(base):
        for j in range(base, base + per):
            pltpu.make_async_copy(w_in.at[j], w_in.at[j], win_sem.at[j]).wait()

    arrived(0)
    for j in range(per):
        acc = dot(normed[local, :], w_in[j]) * (math.log2(math.e) / math.sqrt(width // HEADS))
        acc = acc.astype(BF16)
        q_buf[2 * j] = acc[:, :128]
        q_buf[2 * j + 1] = acc[:, 128:]

    pl.when(late)(share_hidden)

    def keys_values(base, buf):
        arrived(base)
        for j in range(per):
            acc = dot(normed[local, :], w_in[base + j]).astype(BF16)
            buf[2 * j, local, :] = acc[:, :128]
            buf[2 * j + 1, local, :] = acc[:, 128:]

    keys_values(per, k_buf)
    keys_values(2 * per, v_buf)

    span = 256
    low_half = lax.broadcasted_iota(jnp.int32, (PAIR, 128), 1) < 64
    ones = jnp.ones((span, 128), BF16)
    key_at = lax.broadcasted_iota(jnp.int32, (PAIR, span), 1)
    block_at = lax.broadcasted_iota(jnp.int32, (PAIR, span), 0) // BLOCK * BLOCK
    window = (key_at >= block_at) & (key_at < block_at + 4 * BLOCK)

    def bias_of(p):
        usable = window
        if p == 0:
            usable = usable & ((key_at >= LEFT) | (tm > 0))
        if p == pairs - 1:
            usable = usable & ((key_at < LEFT + PAIR) | (tm < n_tm - 1))
        return jnp.where(usable, 0.0, MASKED)

    def attend(members):
        biases = {p: bias_of(p) for p in members}
        steps = [(p, g) for p in members for g in range(groups)]
        scores, raised = {}, {}

        def score(step):
            p, g = step
            q = q_buf[g, pl.ds(p * PAIR, PAIR), :]
            zero = jnp.zeros_like(q)
            q = jnp.concatenate([jnp.where(low_half, q, zero), jnp.where(low_half, zero, q)], axis=0)
            s = dot(q, jnp.transpose(k_buf[g, pl.ds(p * PAIR, span), :]))
            return jnp.concatenate([s[:PAIR] + biases[p], s[PAIR:] + biases[p]], axis=0)

        def raise_to(s):
            return jnp.exp2(s - jnp.max(s, axis=1, keepdims=True)).astype(BF16)

        def combine(step, weights):
            p, g = step
            v = jnp.concatenate([v_buf[g, pl.ds(p * PAIR, span), :], ones], axis=1)
            result = dot(weights, v)
            numer = jnp.where(low_half, result[:PAIR, :128], result[PAIR:, :128])
            denom = jnp.where(low_half, result[:PAIR, 128:], result[PAIR:, 128:])
            att[pl.ds(p * PAIR, PAIR), pl.ds(128 * g, 128)] = (numer / denom).astype(BF16)

        for t in range(len(steps) + 2):
            if t < len(steps):
                scores[t] = score(steps[t])
            if 0 <= t - 1 < len(steps):
                raised[t - 1] = raise_to(scores.pop(t - 1))
            if t >= 2:
                combine(steps[t - 2], raised.pop(t - 2))

    gate_row = mod[2:3, :]

    def project(starts, rows):
        def rows_of(ref, offset=0):
            return jnp.concatenate([ref[pl.ds(s + offset, rows), :] for s in starts], axis=0)
        for c in range(width // 256):
            cols = pl.ds(256 * c, 256)
            mixed = dot(rows_of(att), w_out[:, cols])
            held = jnp.concatenate(
                [hid[pl.ds(LEFT + s, rows), cols] for s in starts], axis=0).astype(F32)
            upd[:, cols] = (held + gate_row[:, 256 * c : 256 * c + 256] * mixed).astype(BF16)
        result = dot(upd[...], w_voc[...]).astype(BF16)
        for at, s in enumerate(starts):
            own[pl.ds(s, rows), :] = result[at * rows : (at + 1) * rows]

    quarter = frames // 4
    last, first = pl.ds(frames - RIM, RIM), pl.ds(0, RIM)
    before, after = pl.ds(lanes - RIM, RIM), pl.ds(frames, RIM)
    rightward = (transfer(2, own.at[last], own.at[before], right),
                 transfer(3, own.at[last], par.at[before], right_partner))
    leftward = (transfer(4, own.at[first], own.at[after], left),
                transfer(5, own.at[first], par.at[after], left_partner))
    shared = [transfer(i, own.at[pl.ds(s, n)], par.at[pl.ds(s, n)], partner)
              for i, s, n in ((6, 3 * quarter, quarter), (7, 0, quarter), (8, quarter, 2 * quarter))]

    wout_copy.wait()
    wvoc_copy.wait()

    def inner_half():
        attend([pairs // 4 + i for i in range(pairs // 2)])
        project((quarter,), 2 * quarter)
        start(shared[2])

    pl.when(late)(inner_half)

    pl.when(has_left)(lambda: wait((to_left,), (to_right,)))
    pl.when(has_right)(lambda: wait((to_right,), (to_left,)))
    normalise(0, LEFT)
    normalise(LEFT + frames, BLOCK)
    rim_rows = jnp.concatenate(
        [normed[pl.ds(0, LEFT), :], normed[pl.ds(LEFT + frames, BLOCK), :]], axis=0)

    def rim_keys_values(base, buf):
        for j in range(per):
            acc = dot(rim_rows, w_in[base + j]).astype(BF16)
            for side in range(2):
                part = acc[:, 128 * side : 128 * side + 128]
                buf[2 * j + side, pl.ds(0, LEFT), :] = part[:LEFT]
                buf[2 * j + side, pl.ds(LEFT + frames, BLOCK), :] = part[LEFT:]

    rim_keys_values(per, k_buf)
    rim_keys_values(2 * per, v_buf)

    attend([(3 * pairs // 4 + i) % pairs for i in range(pairs // 2)])
    project((3 * quarter, 0), quarter)
    pl.when(has_right)(lambda: start(*rightward))
    pl.when(has_left)(lambda: start(*leftward))
    start(*shared[:2])

    pl.when(prompt)(inner_half)

    taps_copy.wait()
    alpha_copy.wait()
    pick_row = lax.broadcasted_iota(jnp.int32, (half, 2 * half), 0)
    pick_col = lax.broadcasted_iota(jnp.int32, (half, 2 * half), 1)
    picked = pick_col == pick_row + parity * half
    for k in range(4):
        taps_t[pl.ds(k * half, half), :] = taps[k, pl.ds(pl.multiple_of(parity * half, half), half), :]
    rate = jnp.sum(jnp.where(picked, alpha[...], 0.0), axis=1, keepdims=True)

    pl.when(has_right)(lambda: wait(rightward, leftward))
    pl.when(has_left)(lambda: wait(leftward, rightward))
    wait(shared, shared)

    own_is_cond = branch_ids[member] == 0
    strength = guidance[member // 2]
    own_weight = jnp.where(own_is_cond, strength, 1.0 - strength)
    par_weight = jnp.where(own_is_cond, 1.0 - strength, strength)
    frame_row = lax.broadcasted_iota(jnp.int32, (lanes, 1), 0)
    frame_row = jnp.where(frame_row < frames + 2 * RIM, frame_row, frame_row - lanes) + tm * frames
    inside = (frame_row >= 0) & (frame_row < total_frames)
    mixed = own_weight * own[...].astype(F32) + par_weight * par[...].astype(F32)
    guided[...] = jnp.where(inside, mixed, 0.0).astype(BF16)

    y_buf[...] = nt_dot(taps_t[...], guided[...])

    frame_lane = lax.broadcasted_iota(jnp.int32, (8, lanes), 1)
    frame_lane = jnp.where(frame_lane < frames + 2 * RIM, frame_lane, frame_lane - lanes) + tm * frames
    kept = (frame_lane >= 0) & (frame_lane < total_frames)

    def ahead(x, count):
        return pltpu.roll(x, (-count) % lanes, 1)

    for c in range(half // 8):
        rate_c = rate[8 * c : 8 * c + 8]
        turn = rate_c * (1.0 / math.pi)
        inverse = 1.0 / rate_c

        def snake(z):
            t = turn * z
            f = t - jnp.round(t)
            u = f * f
            s = SIN2[5]
            for a in (4, 3, 2, 1, 0):
                s = s * u + SIN2[a]
            return z + (s * u) * inverse

        y = [y_buf[pl.ds(k * half + 8 * c, 8), :] for k in range(4)]
        even = jnp.where(kept, y[1] + ahead(y[3], -1), 0.0)
        odd = jnp.where(kept, ahead(y[0], 1) + y[2], 0.0)
        even_p, odd_m = ahead(even, 1), ahead(odd, -1)
        b0, b1, b2, b3, b4, b5 = HALF_BAND
        between_even = (b0 * ahead(even, -1) + b1 * odd_m + b2 * even + b3 * odd
                        + b4 * even_p + b5 * ahead(odd, 1))
        between_odd = (b0 * odd_m + b1 * even + b2 * odd + b3 * even_p
                       + b4 * ahead(odd, 1) + b5 * ahead(even, 2))
        s_even = jnp.where(kept, snake(between_even), 0.0)
        s_odd = jnp.where(kept, snake(between_odd), 0.0)
        l0, l1, l2, l3, l4, l5 = LOW_PASS
        s_even_m, s_odd_m = ahead(s_even, -1), ahead(s_odd, -1)
        s_even_p, s_odd_p = ahead(s_even, 1), ahead(s_odd, 1)
        w_even = (CENTER_TAP * snake(even) + l0 * ahead(s_odd, -2) + l1 * s_even_m + l2 * s_odd_m
                  + l3 * s_even + l4 * s_odd + l5 * s_even_p)
        w_odd = (CENTER_TAP * snake(odd) + l0 * s_even_m + l1 * s_odd_m + l2 * s_even
                 + l3 * s_odd + l4 * s_even_p + l5 * s_odd_p)
        for b in range(frames // 128):
            wave[pl.ds(8 * c, 8), pl.ds(256 * b, 128)] = w_even[:, 128 * b : 128 * b + 128]
            wave[pl.ds(8 * c, 8), pl.ds(256 * b + 128, 128)] = w_odd[:, 128 * b : 128 * b + 128]

    for b in range(frames // 128):
        cols = pl.ds(256 * b, 256)
        out[:, cols] = dot(wave[:, cols].astype(BF16), perm[...]).astype(BF16)


def on_device(hidden_rows, modulation, project_in, project_out, to_vocoder, upsample_taps,
              snake_alpha, guidance, branch_ids):
    n_tm = lax.axis_size("tm")
    _, frames, width = hidden_rows.shape
    cin, cout = upsample_taps.shape[1:]
    half = cout // 2
    extent = LEFT + frames + BLOCK
    held = (frames // PAIR - 1) * PAIR + 256
    groups = width // 128
    lanes = -(-(frames + 2 * RIM) // 128) * 128
    any_spec = pl.BlockSpec(memory_space=pl.ANY)
    smem = pl.BlockSpec(memory_space=pltpu.SMEM)
    return pl.pallas_call(
        functools.partial(kernel, n_tm),
        out_shape=pltpu.VMEM((half, 2 * frames), BF16),
        in_specs=[any_spec] * 7 + [smem] * 2,
        out_specs=pl.BlockSpec(memory_space=pltpu.VMEM),
        scratch_shapes=[
            pltpu.VMEM((extent, width), BF16),
            pltpu.VMEM((extent, width), BF16),
            pltpu.VMEM((3 * width // 256, width, 256), BF16),
            pltpu.VMEM((width, width), BF16),
            pltpu.VMEM((width, cin), BF16),
            pltpu.VMEM((4, cout, cin), BF16),
            pltpu.VMEM((3, width), F32),
            pltpu.VMEM((1, cout), F32),
            pltpu.VMEM((groups, frames, 128), BF16),
            pltpu.VMEM((groups, held, 128), BF16),
            pltpu.VMEM((groups, held, 128), BF16),
            pltpu.VMEM((frames, width), BF16),
            pltpu.VMEM((frames // 2, width), BF16),
            pltpu.VMEM((lanes, cin), BF16),
            pltpu.VMEM((lanes, cin), BF16),
            pltpu.VMEM((lanes, cin), BF16),
            pltpu.VMEM((4 * half, lanes), F32),
            pltpu.VMEM((half, 2 * frames), F32),
            pltpu.VMEM((4 * half, cin), BF16),
            pltpu.VMEM((256, 256), BF16),
            pltpu.SemaphoreType.DMA((4,)),
            pltpu.SemaphoreType.DMA((3 * width // 256,)),
            pltpu.SemaphoreType.DMA((5,)),
            pltpu.SemaphoreType.DMA((9,)),
            pltpu.SemaphoreType.DMA((9,)),
        ],
        compiler_params=pltpu.CompilerParams(
            collective_id=0, has_side_effects=True, vmem_limit_bytes=56 * 1024 * 1024),
        cost_estimate=pl.CostEstimate(
            flops=9_000_000_000, bytes_accessed=12_000_000, transcendentals=3_000_000),
    )(hidden_rows, modulation.transpose(1, 0, 2), project_in, project_out, to_vocoder,
      upsample_taps.transpose(0, 2, 1), snake_alpha[None, :], guidance, branch_ids)


def solution(mesh):
    in_specs = (P("guide", "tm", None), P("guide", None, None), P(), P(), P(), P(), P(), P(), P())
    return jax.shard_map(
        on_device, mesh=mesh, in_specs=in_specs, out_specs=P("guide", "tm"), check_vma=False)
```

```python
import functools
import math

import jax
import jax.numpy as jnp
from jax import lax
from jax.experimental import pallas as pl
from jax.experimental.pallas import tpu as pltpu
from jax.sharding import PartitionSpec as P

HEADS = 16
BLOCK = 48
HALF_BAND = (3.0 / 256.0, -25.0 / 256.0, 150.0 / 256.0, 150.0 / 256.0, -25.0 / 256.0, 3.0 / 256.0)
LOW_PASS = (0.012, -0.06, 0.3, 0.3, -0.06, 0.012)
CENTER_TAP = 0.5
SIN2 = (9.869604202977849, -32.469663586217976, 42.72706432039706,
        -30.100639734504547, 13.048356860034854, -3.3563323291898937)
MASKED = -1e30
MESH = pl.DeviceIdType.MESH
F32 = jnp.float32
BF16 = jnp.bfloat16

PAIR = 2 * BLOCK
LEFT = 2 * BLOCK
RING = 4
RIM = 16


def nt_dot(a, b):
    return lax.dot_general(a, b, (((1,), (1,)), ((), ())), preferred_element_type=F32)


def dot(a, b):
    return jnp.dot(a, b, preferred_element_type=F32)


def kernel(n_tm, hidden, modulation, w_in_hbm, w_out_hbm, w_voc_hbm, taps_hbm, alpha_hbm,
           guidance, branch_ids, out,
           hid, normed, w_in, w_out, w_voc, taps, mod, alpha,
           q_buf, k_buf, v_buf, att, upd, own, par, guided, y_buf, wave, taps_t, perm,
           hid_sem, win_sem, in_sem, send_sem, recv_sem):
    frames = hidden.shape[1]
    width = hidden.shape[2]
    pairs = frames // PAIR
    groups = width // 128
    extent = LEFT + frames + BLOCK
    half = out.shape[0]
    lanes = own.shape[0]
    cin = own.shape[1]
    total_frames = n_tm * frames

    tm = lax.axis_index("tm")
    member = lax.axis_index("guide")
    parity = lax.rem(member, 2)
    other = member + 1 - 2 * parity
    has_left, has_right = tm > 0, tm < n_tm - 1
    deferred = tm == n_tm // 2
    late = deferred | (tm == n_tm // 2 + 1)
    prompt = jnp.logical_not(late)
    split = deferred | (tm == n_tm // 2 - 1)
    whole = jnp.logical_not(split)
    eager = lax.rem(tm, RING) == RING - 1
    left_tm, right_tm = jnp.maximum(tm - 1, 0), jnp.minimum(tm + 1, n_tm - 1)
    left, right = (left_tm, member), (right_tm, member)
    partner = (tm, other)
    left_partner, right_partner = (left_tm, other), (right_tm, other)

    barrier = pltpu.get_barrier_semaphore()

    def greet(*devices):
        for device in devices:
            pl.semaphore_signal(barrier, inc=1, device_id=device, device_id_type=MESH)

    greet(partner)
    pl.when(has_left)(lambda: greet(left, left_partner))
    pl.when(has_right)(lambda: greet(right, right_partner))

    def load(src, dst, sem):
        copy = pltpu.make_async_copy(src, dst, sem)
        copy.start()
        return copy

    parts = 4
    part = frames // parts
    hid_copies = [load(hidden.at[0, pl.ds(part * i, part)], hid.at[pl.ds(LEFT + part * i, part)],
                       hid_sem.at[i]) for i in range(parts)]
    mod_copy = load(modulation.at[:, 0], mod, in_sem.at[0])

    def transfer(i, src, dst, device):
        return pltpu.make_async_remote_copy(
            src_ref=src, dst_ref=dst, send_sem=send_sem.at[i], recv_sem=recv_sem.at[i],
            device_id=device, device_id_type=MESH)

    def start(*copies):
        for copy in copies:
            copy.start()

    def wait(sent, received):
        for copy in sent:
            copy.wait_send()
        for copy in received:
            copy.wait_recv()

    to_right = transfer(0, hidden.at[0, pl.ds(frames - LEFT, LEFT)], hid.at[pl.ds(0, LEFT)], right)
    to_left = transfer(1, hidden.at[0, pl.ds(0, BLOCK)], hid.at[pl.ds(LEFT + frames, BLOCK)], left)

    def share_hidden():
        pl.semaphore_wait(
            barrier, 1 + 2 * has_left.astype(jnp.int32) + 2 * has_right.astype(jnp.int32))
        pl.when(has_right)(lambda: start(to_right))
        pl.when(has_left)(lambda: start(to_left))

    pl.when(eager)(share_hidden)

    def load_weights():
        tiles = w_in.shape[0]
        copies = [load(w_in_hbm.at[:, pl.ds(256 * j, 256)], w_in.at[j], win_sem.at[j])
                  for j in range(tiles)]
        for i, (src, dst) in enumerate(((w_out_hbm, w_out), (w_voc_hbm, w_voc),
                                        (taps_hbm, taps), (alpha_hbm, alpha))):
            copies.append(load(src, dst, in_sem.at[i + 1]))
        return copies[tiles:]

    hid_copies[0].wait()
    wout_copy, wvoc_copy, taps_copy, alpha_copy = load_weights()

    spare = k_buf.shape[1] - extent
    k_buf[:, pl.ds(extent, spare), :] = jnp.zeros((groups, spare, 128), BF16)
    v_buf[:, pl.ds(extent, spare), :] = jnp.zeros((groups, spare, 128), BF16)
    gap = lanes - frames - 2 * RIM

    def clear(start, count):
        own[pl.ds(start, count), :] = jnp.zeros((count, cin), BF16)
        par[pl.ds(start, count), :] = jnp.zeros((count, cin), BF16)

    clear(frames + RIM, gap)

    @pl.when(tm == 0)
    def _():
        hid[pl.ds(0, LEFT), :] = jnp.zeros((LEFT, width), BF16)
        clear(lanes - RIM, RIM)

    @pl.when(tm == n_tm - 1)
    def _():
        hid[pl.ds(LEFT + frames, BLOCK), :] = jnp.zeros((BLOCK, width), BF16)
        clear(frames, RIM)

    row = lax.broadcasted_iota(jnp.int32, (256, 256), 0)
    col = lax.broadcasted_iota(jnp.int32, (256, 256), 1)
    perm[...] = jnp.where(row == (col % 2) * 128 + col // 2, 1.0, 0.0).astype(BF16)

    mod_copy.wait()
    scale_row = 1.0 + mod[0:1, :]
    shift_row = mod[1:2, :]

    def normalise(start, rows):
        x = hid[pl.ds(start, rows), :].astype(F32)
        centered = x - jnp.mean(x, axis=-1, keepdims=True)
        variance = jnp.mean(centered * centered, axis=-1, keepdims=True)
        result = centered * lax.rsqrt(variance + 1e-6) * scale_row + shift_row
        normed[pl.ds(start, rows), :] = result.astype(BF16)

    for i in range(parts):
        if i > 0:
            hid_copies[i].wait()

        def norm_step(j, carry):
            normalise(pl.multiple_of(LEFT + i * part + j * PAIR, PAIR), PAIR)
            return carry

        lax.fori_loop(0, part // PAIR, norm_step, 0)
        if i == 1:
            pl.when(jnp.logical_not(deferred | eager))(share_hidden)

    per = groups // 2
    local = pl.ds(LEFT, frames)

    def arrived(base):
        for j in range(base, base + per):
            pltpu.make_async_copy(w_in.at[j], w_in.at[j], win_sem.at[j]).wait()

    arrived(0)
    for j in range(per):
        acc = dot(normed[local, :], w_in[j]) * (math.log2(math.e) / math.sqrt(width // HEADS))
        acc = acc.astype(BF16)
        q_buf[2 * j] = acc[:, :128]
        q_buf[2 * j + 1] = acc[:, 128:]

    def keys_values(base, buf, tiles):
        for j in tiles:
            acc = dot(normed[local, :], w_in[base + j]).astype(BF16)
            buf[2 * j, local, :] = acc[:, :128]
            buf[2 * j + 1, local, :] = acc[:, 128:]

    arrived(per)
    arrived(2 * per)
    keys_values(per, k_buf, range(per))
    keys_values(2 * per, v_buf, range(per // 2))
    pl.when(deferred)(share_hidden)
    keys_values(2 * per, v_buf, range(per // 2, per))

    span = 256
    low_half = lax.broadcasted_iota(jnp.int32, (PAIR, 128), 1) < 64
    ones = jnp.ones((span, 128), BF16)
    key_at = lax.broadcasted_iota(jnp.int32, (PAIR, span), 1)
    block_at = lax.broadcasted_iota(jnp.int32, (PAIR, span), 0) // BLOCK * BLOCK
    window = (key_at >= block_at) & (key_at < block_at + 4 * BLOCK)

    def bias_of(p):
        usable = window
        if p == 0:
            usable = usable & ((key_at >= LEFT) | (tm > 0))
        if p == pairs - 1:
            usable = usable & ((key_at < LEFT + PAIR) | (tm < n_tm - 1))
        return jnp.where(usable, 0.0, MASKED)

    def attend(members):
        biases = {p: bias_of(p) for p in members}
        steps = [(p, g) for p in members for g in range(groups)]
        scores, raised = {}, {}

        def score(step):
            p, g = step
            q = q_buf[g, pl.ds(p * PAIR, PAIR), :]
            zero = jnp.zeros_like(q)
            q = jnp.concatenate([jnp.where(low_half, q, zero), jnp.where(low_half, zero, q)], axis=0)
            s = dot(q, jnp.transpose(k_buf[g, pl.ds(p * PAIR, span), :]))
            return jnp.concatenate([s[:PAIR] + biases[p], s[PAIR:] + biases[p]], axis=0)

        def raise_to(s):
            return jnp.exp2(s - jnp.max(s, axis=1, keepdims=True)).astype(BF16)

        def combine(step, weights):
            p, g = step
            v = jnp.concatenate([v_buf[g, pl.ds(p * PAIR, span), :], ones], axis=1)
            result = dot(weights, v)
            numer = jnp.where(low_half, result[:PAIR, :128], result[PAIR:, :128])
            denom = jnp.where(low_half, result[:PAIR, 128:], result[PAIR:, 128:])
            att[pl.ds(p * PAIR, PAIR), pl.ds(128 * g, 128)] = (numer / denom).astype(BF16)

        for t in range(len(steps) + 2):
            if t < len(steps):
                scores[t] = score(steps[t])
            if 0 <= t - 1 < len(steps):
                raised[t - 1] = raise_to(scores.pop(t - 1))
            if t >= 2:
                combine(steps[t - 2], raised.pop(t - 2))

    gate_row = mod[2:3, :]

    def project(starts, rows):
        count = rows * len(starts)
        def rows_of(ref, offset=0):
            return jnp.concatenate([ref[pl.ds(s + offset, rows), :] for s in starts], axis=0)
        for c in range(width // 256):
            cols = pl.ds(256 * c, 256)
            mixed = dot(rows_of(att), w_out[:, cols])
            held = jnp.concatenate(
                [hid[pl.ds(LEFT + s, rows), cols] for s in starts], axis=0).astype(F32)
            upd[pl.ds(0, count), cols] = (held + gate_row[:, 256 * c : 256 * c + 256] * mixed).astype(BF16)
        result = dot(upd[pl.ds(0, count), :], w_voc[...]).astype(BF16)
        for at, s in enumerate(starts):
            own[pl.ds(s, rows), :] = result[at * rows : (at + 1) * rows]

    quarter = frames // 4
    last, first = pl.ds(frames - RIM, RIM), pl.ds(0, RIM)
    before, after = pl.ds(lanes - RIM, RIM), pl.ds(frames, RIM)
    rightward = (transfer(2, own.at[last], own.at[before], right),
                 transfer(3, own.at[last], par.at[before], right_partner))
    leftward = (transfer(4, own.at[first], own.at[after], left),
                transfer(5, own.at[first], par.at[after], left_partner))
    shared = [transfer(i, own.at[pl.ds(s, n)], par.at[pl.ds(s, n)], partner)
              for i, s, n in ((6, 3 * quarter, quarter), (7, 0, quarter), (8, quarter, 2 * quarter),
                              (6, PAIR, frames - 2 * PAIR), (7, frames - PAIR, PAIR), (8, 0, PAIR))]

    wout_copy.wait()
    wvoc_copy.wait()

    @pl.when(late)
    def _():
        attend([i for i in range(1, pairs - 1)])
        project((PAIR,), frames - 2 * PAIR)
        start(shared[3])

    pl.when(has_left)(lambda: wait((to_left,), (to_right,)))
    pl.when(has_right)(lambda: wait((to_right,), (to_left,)))
    normalise(0, LEFT)
    normalise(LEFT + frames, BLOCK)
    rim_rows = jnp.concatenate(
        [normed[pl.ds(0, LEFT), :], normed[pl.ds(LEFT + frames, BLOCK), :]], axis=0)

    def rim_keys_values(base, buf):
        for j in range(per):
            acc = dot(rim_rows, w_in[base + j]).astype(BF16)
            for side in range(2):
                part = acc[:, 128 * side : 128 * side + 128]
                buf[2 * j + side, pl.ds(0, LEFT), :] = part[:LEFT]
                buf[2 * j + side, pl.ds(LEFT + frames, BLOCK), :] = part[LEFT:]

    rim_keys_values(per, k_buf)
    rim_keys_values(2 * per, v_buf)

    def send_rims():
        pl.when(has_right)(lambda: start(*rightward))
        pl.when(has_left)(lambda: start(*leftward))

    @pl.when(late)
    def _():
        attend([pairs - 1, 0])
        project((frames - PAIR, 0), PAIR)
        send_rims()
        start(*shared[4:])

    @pl.when(prompt)
    def _():
        attend([(3 * pairs // 4 + i) % pairs for i in range(pairs // 2)])
        project((3 * quarter, 0), quarter)
        send_rims()
        start(*shared[:2])
        attend([pairs // 4 + i for i in range(pairs // 2)])
        project((quarter,), 2 * quarter)
        start(shared[2])

    taps_copy.wait()
    alpha_copy.wait()
    pick_row = lax.broadcasted_iota(jnp.int32, (half, 2 * half), 0)
    pick_col = lax.broadcasted_iota(jnp.int32, (half, 2 * half), 1)
    picked = pick_col == pick_row + parity * half
    for k in range(4):
        taps_t[pl.ds(k * half, half), :] = taps[k, pl.ds(pl.multiple_of(parity * half, half), half), :]
    rate = jnp.sum(jnp.where(picked, alpha[...], 0.0), axis=1, keepdims=True)

    def rims_arrived():
        pl.when(has_right)(lambda: wait(rightward, leftward))
        pl.when(has_left)(lambda: wait(leftward, rightward))

    pl.when(prompt)(lambda: wait(shared[:3], shared[:3]))
    pl.when(late)(lambda: wait(shared[3:], shared[3:]))

    own_is_cond = branch_ids[member] == 0
    strength = guidance[member // 2]
    own_weight = jnp.where(own_is_cond, strength, 1.0 - strength)
    par_weight = jnp.where(own_is_cond, 1.0 - strength, strength)
    def frame_of(at):
        return jnp.where(at < frames + 2 * RIM, at, at - lanes) + tm * frames

    def mix(start, rows):
        frame = frame_of(lax.broadcasted_iota(jnp.int32, (rows, 1), 0) + start)
        inside = (frame >= 0) & (frame < total_frames)
        part = pl.ds(start, rows)
        mixed = own_weight * own[part, :].astype(F32) + par_weight * par[part, :].astype(F32)
        guided[part, :] = jnp.where(inside, mixed, 0.0).astype(BF16)
        y_buf[:, part] = nt_dot(taps_t[...], guided[part, :])

    def finish(tiles, results):
        extent_lanes = 128 * len(tiles)
        lane_at = lax.broadcasted_iota(jnp.int32, (8, 128), 1)
        frame_lane = frame_of(jnp.concatenate([lane_at + 128 * t for t in tiles], axis=1))
        kept = (frame_lane >= 0) & (frame_lane < total_frames)

        def ahead(x, count):
            return pltpu.roll(x, (-count) % extent_lanes, 1)

        for c in range(half // 8):
            rate_c = rate[8 * c : 8 * c + 8]
            turn = rate_c * (1.0 / math.pi)
            inverse = 1.0 / rate_c

            def snake(z):
                t = turn * z
                f = t - jnp.round(t)
                u = f * f
                s = SIN2[5]
                for a in (4, 3, 2, 1, 0):
                    s = s * u + SIN2[a]
                return z + (s * u) * inverse

            y = [jnp.concatenate([y_buf[pl.ds(k * half + 8 * c, 8), pl.ds(128 * t, 128)] for t in tiles],
                                 axis=1) for k in range(4)]
            even = jnp.where(kept, y[1] + ahead(y[3], -1), 0.0)
            odd = jnp.where(kept, ahead(y[0], 1) + y[2], 0.0)
            even_p, odd_m = ahead(even, 1), ahead(odd, -1)
            b0, b1, b2, b3, b4, b5 = HALF_BAND
            between_even = (b0 * ahead(even, -1) + b1 * odd_m + b2 * even + b3 * odd
                            + b4 * even_p + b5 * ahead(odd, 1))
            between_odd = (b0 * odd_m + b1 * even + b2 * odd + b3 * even_p
                           + b4 * ahead(odd, 1) + b5 * ahead(even, 2))
            s_even = jnp.where(kept, snake(between_even), 0.0)
            s_odd = jnp.where(kept, snake(between_odd), 0.0)
            l0, l1, l2, l3, l4, l5 = LOW_PASS
            s_even_m, s_odd_m = ahead(s_even, -1), ahead(s_odd, -1)
            s_even_p, s_odd_p = ahead(s_even, 1), ahead(s_odd, 1)
            w_even = (CENTER_TAP * snake(even) + l0 * ahead(s_odd, -2) + l1 * s_even_m + l2 * s_odd_m
                      + l3 * s_even + l4 * s_odd + l5 * s_even_p)
            w_odd = (CENTER_TAP * snake(odd) + l0 * s_even_m + l1 * s_odd_m + l2 * s_even
                     + l3 * s_odd + l4 * s_even_p + l5 * s_odd_p)
            for b in results:
                at = 128 * tiles.index(b)
                wave[pl.ds(8 * c, 8), pl.ds(256 * b, 128)] = w_even[:, at : at + 128]
                wave[pl.ds(8 * c, 8), pl.ds(256 * b + 128, 128)] = w_odd[:, at : at + 128]

        for b in results:
            cols = pl.ds(256 * b, 256)
            out[:, cols] = dot(wave[:, cols].astype(BF16), perm[...]).astype(BF16)


    n_tiles = lanes // 128
    out_tiles = frames // 128

    @pl.when(whole)
    def _():
        rims_arrived()
        mix(0, lanes)
        finish(list(range(n_tiles)), list(range(out_tiles)))

    @pl.when(split)
    def _():
        mix(0, frames)
        finish(list(range(out_tiles)), list(range(1, out_tiles - 1)))
        rims_arrived()
        mix(frames, lanes - frames)
        finish(list(range(out_tiles - 2, n_tiles)) + [0, 1], [out_tiles - 1, 0])


def on_device(hidden_rows, modulation, project_in, project_out, to_vocoder, upsample_taps,
              snake_alpha, guidance, branch_ids):
    n_tm = lax.axis_size("tm")
    _, frames, width = hidden_rows.shape
    cin, cout = upsample_taps.shape[1:]
    half = cout // 2
    extent = LEFT + frames + BLOCK
    held = (frames // PAIR - 1) * PAIR + 256
    groups = width // 128
    lanes = -(-(frames + 2 * RIM) // 128) * 128
    any_spec = pl.BlockSpec(memory_space=pl.ANY)
    smem = pl.BlockSpec(memory_space=pltpu.SMEM)
    return pl.pallas_call(
        functools.partial(kernel, n_tm),
        out_shape=pltpu.VMEM((half, 2 * frames), BF16),
        in_specs=[any_spec] * 7 + [smem] * 2,
        out_specs=pl.BlockSpec(memory_space=pltpu.VMEM),
        scratch_shapes=[
            pltpu.VMEM((extent, width), BF16),
            pltpu.VMEM((extent, width), BF16),
            pltpu.VMEM((3 * width // 256, width, 256), BF16),
            pltpu.VMEM((width, width), BF16),
            pltpu.VMEM((width, cin), BF16),
            pltpu.VMEM((4, cout, cin), BF16),
            pltpu.VMEM((3, width), F32),
            pltpu.VMEM((1, cout), F32),
            pltpu.VMEM((groups, frames, 128), BF16),
            pltpu.VMEM((groups, held, 128), BF16),
            pltpu.VMEM((groups, held, 128), BF16),
            pltpu.VMEM((frames, width), BF16),
            pltpu.VMEM((frames, width), BF16),
            pltpu.VMEM((lanes, cin), BF16),
            pltpu.VMEM((lanes, cin), BF16),
            pltpu.VMEM((lanes, cin), BF16),
            pltpu.VMEM((4 * half, lanes), F32),
            pltpu.VMEM((half, 2 * frames), F32),
            pltpu.VMEM((4 * half, cin), BF16),
            pltpu.VMEM((256, 256), BF16),
            pltpu.SemaphoreType.DMA((4,)),
            pltpu.SemaphoreType.DMA((3 * width // 256,)),
            pltpu.SemaphoreType.DMA((5,)),
            pltpu.SemaphoreType.DMA((9,)),
            pltpu.SemaphoreType.DMA((9,)),
        ],
        compiler_params=pltpu.CompilerParams(
            collective_id=0, has_side_effects=True, vmem_limit_bytes=56 * 1024 * 1024),
        cost_estimate=pl.CostEstimate(
            flops=9_000_000_000, bytes_accessed=12_000_000, transcendentals=3_000_000),
    )(hidden_rows, modulation.transpose(1, 0, 2), project_in, project_out, to_vocoder,
      upsample_taps.transpose(0, 2, 1), snake_alpha[None, :], guidance, branch_ids)


def solution(mesh):
    in_specs = (P("guide", "tm", None), P("guide", None, None), P(), P(), P(), P(), P(), P(), P())
    return jax.shard_map(
        on_device, mesh=mesh, in_specs=in_specs, out_specs=P("guide", "tm"), check_vma=False)
```

```python
import functools
import math

import jax
import jax.numpy as jnp
from jax import lax
from jax.experimental import pallas as pl
from jax.experimental.pallas import tpu as pltpu
from jax.sharding import PartitionSpec as P

HEADS = 16
BLOCK = 48
HALF_BAND = (3.0 / 256.0, -25.0 / 256.0, 150.0 / 256.0, 150.0 / 256.0, -25.0 / 256.0, 3.0 / 256.0)
LOW_PASS = (0.012, -0.06, 0.3, 0.3, -0.06, 0.012)
CENTER_TAP = 0.5
SIN2 = (9.869604202977849, -32.469663586217976, 42.72706432039706,
        -30.100639734504547, 13.048356860034854, -3.3563323291898937)
MASKED = -1e30
MESH = pl.DeviceIdType.MESH
F32 = jnp.float32
BF16 = jnp.bfloat16

PAIR = 2 * BLOCK
LEFT = 2 * BLOCK
RING = 4
RIM = 16


def nt_dot(a, b):
    return lax.dot_general(a, b, (((1,), (1,)), ((), ())), preferred_element_type=F32)


def dot(a, b):
    return jnp.dot(a, b, preferred_element_type=F32)


def kernel(n_tm, hidden, modulation, w_in_hbm, w_out_hbm, w_voc_hbm, taps_hbm, alpha_hbm,
           guidance, branch_ids, out,
           hid, normed, w_in, w_out, w_voc, taps, mod, alpha,
           q_buf, k_buf, v_buf, att, upd, own, par, guided, y_buf, wave, taps_t, perm,
           hid_sem, win_sem, in_sem, send_sem, recv_sem):
    frames = hidden.shape[1]
    width = hidden.shape[2]
    pairs = frames // PAIR
    groups = width // 128
    extent = LEFT + frames + BLOCK
    half = out.shape[0]
    lanes = own.shape[0]
    cin = own.shape[1]
    total_frames = n_tm * frames

    tm = lax.axis_index("tm")
    member = lax.axis_index("guide")
    parity = lax.rem(member, 2)
    other = member + 1 - 2 * parity
    has_left, has_right = tm > 0, tm < n_tm - 1
    deferred = tm == n_tm // 2
    late = deferred | (tm == n_tm // 2 + 1)
    leader = tm == n_tm // 2 - 1
    prompt = jnp.logical_not(late | leader)
    split = deferred | leader
    whole = jnp.logical_not(split)
    eager = lax.rem(tm, RING) == RING - 1
    left_tm, right_tm = jnp.maximum(tm - 1, 0), jnp.minimum(tm + 1, n_tm - 1)
    left, right = (left_tm, member), (right_tm, member)
    partner = (tm, other)
    left_partner, right_partner = (left_tm, other), (right_tm, other)

    barrier = pltpu.get_barrier_semaphore()

    def greet(*devices):
        for device in devices:
            pl.semaphore_signal(barrier, inc=1, device_id=device, device_id_type=MESH)

    greet(partner)
    pl.when(has_left)(lambda: greet(left, left_partner))
    pl.when(has_right)(lambda: greet(right, right_partner))

    def load(src, dst, sem):
        copy = pltpu.make_async_copy(src, dst, sem)
        copy.start()
        return copy

    parts = 4
    part = frames // parts
    hid_copies = [load(hidden.at[0, pl.ds(part * i, part)], hid.at[pl.ds(LEFT + part * i, part)],
                       hid_sem.at[i]) for i in range(parts)]
    mod_copy = load(modulation.at[:, 0], mod, in_sem.at[0])

    def transfer(i, src, dst, device):
        return pltpu.make_async_remote_copy(
            src_ref=src, dst_ref=dst, send_sem=send_sem.at[i], recv_sem=recv_sem.at[i],
            device_id=device, device_id_type=MESH)

    def start(*copies):
        for copy in copies:
            copy.start()

    def wait(sent, received):
        for copy in sent:
            copy.wait_send()
        for copy in received:
            copy.wait_recv()

    to_right = transfer(0, hidden.at[0, pl.ds(frames - LEFT, LEFT)], hid.at[pl.ds(0, LEFT)], right)
    to_left = transfer(1, hidden.at[0, pl.ds(0, BLOCK)], hid.at[pl.ds(LEFT + frames, BLOCK)], left)

    def share_hidden(left_first=False):
        pl.semaphore_wait(
            barrier, 1 + 2 * has_left.astype(jnp.int32) + 2 * has_right.astype(jnp.int32))
        if left_first:
            pl.when(has_left)(lambda: start(to_left))
        pl.when(has_right)(lambda: start(to_right))
        if not left_first:
            pl.when(has_left)(lambda: start(to_left))

    pl.when(eager)(share_hidden)

    def load_weights():
        tiles = w_in.shape[0]
        copies = [load(w_in_hbm.at[:, pl.ds(256 * j, 256)], w_in.at[j], win_sem.at[j])
                  for j in range(tiles)]
        for i, (src, dst) in enumerate(((w_out_hbm, w_out), (w_voc_hbm, w_voc),
                                        (taps_hbm, taps), (alpha_hbm, alpha))):
            copies.append(load(src, dst, in_sem.at[i + 1]))
        return copies[tiles:]

    hid_copies[0].wait()
    wout_copy, wvoc_copy, taps_copy, alpha_copy = load_weights()

    spare = k_buf.shape[1] - extent
    k_buf[:, pl.ds(extent, spare), :] = jnp.zeros((groups, spare, 128), BF16)
    v_buf[:, pl.ds(extent, spare), :] = jnp.zeros((groups, spare, 128), BF16)
    gap = lanes - frames - 2 * RIM

    def clear(start, count):
        own[pl.ds(start, count), :] = jnp.zeros((count, cin), BF16)
        par[pl.ds(start, count), :] = jnp.zeros((count, cin), BF16)

    clear(frames + RIM, gap)

    @pl.when(tm == 0)
    def _():
        hid[pl.ds(0, LEFT), :] = jnp.zeros((LEFT, width), BF16)
        clear(lanes - RIM, RIM)

    @pl.when(tm == n_tm - 1)
    def _():
        hid[pl.ds(LEFT + frames, BLOCK), :] = jnp.zeros((BLOCK, width), BF16)
        clear(frames, RIM)

    row = lax.broadcasted_iota(jnp.int32, (256, 256), 0)
    col = lax.broadcasted_iota(jnp.int32, (256, 256), 1)
    perm[...] = jnp.where(row == (col % 2) * 128 + col // 2, 1.0, 0.0).astype(BF16)

    mod_copy.wait()
    scale_row = 1.0 + mod[0:1, :]
    shift_row = mod[1:2, :]

    def normalise(start, rows):
        x = hid[pl.ds(start, rows), :].astype(F32)
        centered = x - jnp.mean(x, axis=-1, keepdims=True)
        variance = jnp.mean(centered * centered, axis=-1, keepdims=True)
        result = centered * lax.rsqrt(variance + 1e-6) * scale_row + shift_row
        normed[pl.ds(start, rows), :] = result.astype(BF16)

    for i in range(parts):
        if i > 0:
            hid_copies[i].wait()

        def norm_step(j, carry):
            normalise(pl.multiple_of(LEFT + i * part + j * PAIR, PAIR), PAIR)
            return carry

        lax.fori_loop(0, part // PAIR, norm_step, 0)
        if i == 1:
            pl.when(jnp.logical_not(deferred | eager))(share_hidden)

    per = groups // 2
    local = pl.ds(LEFT, frames)

    def arrived(base):
        for j in range(base, base + per):
            pltpu.make_async_copy(w_in.at[j], w_in.at[j], win_sem.at[j]).wait()

    arrived(0)
    for j in range(per):
        acc = dot(normed[local, :], w_in[j]) * (math.log2(math.e) / math.sqrt(width // HEADS))
        acc = acc.astype(BF16)
        q_buf[2 * j] = acc[:, :128]
        q_buf[2 * j + 1] = acc[:, 128:]

    def keys_values(base, buf, tiles):
        for j in tiles:
            acc = dot(normed[local, :], w_in[base + j]).astype(BF16)
            buf[2 * j, local, :] = acc[:, :128]
            buf[2 * j + 1, local, :] = acc[:, 128:]

    arrived(per)
    arrived(2 * per)
    keys_values(per, k_buf, range(per))
    keys_values(2 * per, v_buf, range(per // 2))
    pl.when(deferred)(lambda: share_hidden(True))
    keys_values(2 * per, v_buf, range(per // 2, per))

    span = 256
    low_half = lax.broadcasted_iota(jnp.int32, (PAIR, 128), 1) < 64
    ones = jnp.ones((span, 128), BF16)
    key_at = lax.broadcasted_iota(jnp.int32, (PAIR, span), 1)
    block_at = lax.broadcasted_iota(jnp.int32, (PAIR, span), 0) // BLOCK * BLOCK
    window = (key_at >= block_at) & (key_at < block_at + 4 * BLOCK)

    def bias_of(p):
        usable = window
        if p == 0:
            usable = usable & ((key_at >= LEFT) | (tm > 0))
        if p == pairs - 1:
            usable = usable & ((key_at < LEFT + PAIR) | (tm < n_tm - 1))
        return jnp.where(usable, 0.0, MASKED)

    def attend(members):
        biases = {p: bias_of(p) for p in members}
        steps = [(p, g) for p in members for g in range(groups)]
        scores, raised = {}, {}

        def score(step):
            p, g = step
            q = q_buf[g, pl.ds(p * PAIR, PAIR), :]
            zero = jnp.zeros_like(q)
            q = jnp.concatenate([jnp.where(low_half, q, zero), jnp.where(low_half, zero, q)], axis=0)
            s = dot(q, jnp.transpose(k_buf[g, pl.ds(p * PAIR, span), :]))
            return jnp.concatenate([s[:PAIR] + biases[p], s[PAIR:] + biases[p]], axis=0)

        def raise_to(s):
            return jnp.exp2(s - jnp.max(s, axis=1, keepdims=True)).astype(BF16)

        def combine(step, weights):
            p, g = step
            v = jnp.concatenate([v_buf[g, pl.ds(p * PAIR, span), :], ones], axis=1)
            result = dot(weights, v)
            numer = jnp.where(low_half, result[:PAIR, :128], result[PAIR:, :128])
            denom = jnp.where(low_half, result[:PAIR, 128:], result[PAIR:, 128:])
            att[pl.ds(p * PAIR, PAIR), pl.ds(128 * g, 128)] = (numer / denom).astype(BF16)

        for t in range(len(steps) + 2):
            if t < len(steps):
                scores[t] = score(steps[t])
            if 0 <= t - 1 < len(steps):
                raised[t - 1] = raise_to(scores.pop(t - 1))
            if t >= 2:
                combine(steps[t - 2], raised.pop(t - 2))

    gate_row = mod[2:3, :]

    def project(starts, rows):
        count = rows * len(starts)
        def rows_of(ref, offset=0):
            return jnp.concatenate([ref[pl.ds(s + offset, rows), :] for s in starts], axis=0)
        for c in range(width // 256):
            cols = pl.ds(256 * c, 256)
            mixed = dot(rows_of(att), w_out[:, cols])
            held = jnp.concatenate(
                [hid[pl.ds(LEFT + s, rows), cols] for s in starts], axis=0).astype(F32)
            upd[pl.ds(0, count), cols] = (held + gate_row[:, 256 * c : 256 * c + 256] * mixed).astype(BF16)
        result = dot(upd[pl.ds(0, count), :], w_voc[...]).astype(BF16)
        for at, s in enumerate(starts):
            own[pl.ds(s, rows), :] = result[at * rows : (at + 1) * rows]

    quarter = frames // 4
    last, first = pl.ds(frames - RIM, RIM), pl.ds(0, RIM)
    before, after = pl.ds(lanes - RIM, RIM), pl.ds(frames, RIM)
    rightward = (transfer(2, own.at[last], own.at[before], right),
                 transfer(3, own.at[last], par.at[before], right_partner))
    leftward = (transfer(4, own.at[first], own.at[after], left),
                transfer(5, own.at[first], par.at[after], left_partner))
    shared = [transfer(i, own.at[pl.ds(s, n)], par.at[pl.ds(s, n)], partner)
              for i, s, n in ((6, 3 * quarter, quarter), (7, 0, quarter), (8, quarter, 2 * quarter),
                              (6, PAIR, frames - 2 * PAIR), (7, frames - PAIR, PAIR), (8, 0, PAIR),
                              (6, 0, frames - PAIR))]

    wout_copy.wait()
    wvoc_copy.wait()

    @pl.when(late)
    def _():
        attend([i for i in range(1, pairs - 1)])
        project((PAIR,), frames - 2 * PAIR)
        start(shared[3])

    @pl.when(leader)
    def _():
        attend([i for i in range(2, pairs - 2)])

    pl.when(has_left)(lambda: wait((to_left,), (to_right,)))
    pl.when(has_right)(lambda: wait((to_right,), (to_left,)))
    normalise(0, LEFT)
    normalise(LEFT + frames, BLOCK)
    rim_rows = jnp.concatenate(
        [normed[pl.ds(0, LEFT), :], normed[pl.ds(LEFT + frames, BLOCK), :]], axis=0)

    def rim_keys_values(base, buf):
        for j in range(per):
            acc = dot(rim_rows, w_in[base + j]).astype(BF16)
            for side in range(2):
                part = acc[:, 128 * side : 128 * side + 128]
                buf[2 * j + side, pl.ds(0, LEFT), :] = part[:LEFT]
                buf[2 * j + side, pl.ds(LEFT + frames, BLOCK), :] = part[LEFT:]

    rim_keys_values(per, k_buf)
    rim_keys_values(2 * per, v_buf)

    def send_rims():
        pl.when(has_right)(lambda: start(*rightward))
        pl.when(has_left)(lambda: start(*leftward))

    @pl.when(late)
    def _():
        attend([pairs - 1, 0])
        project((frames - PAIR, 0), PAIR)
        send_rims()
        start(*shared[4:6])

    @pl.when(leader)
    def _():
        attend([pairs - 1])
        project((frames - PAIR,), PAIR)
        pl.when(has_right)(lambda: start(*rightward))
        start(shared[4])
        attend([0, 1, pairs - 2])
        project((0,), frames - PAIR)
        pl.when(has_left)(lambda: start(*leftward))
        start(shared[6])

    @pl.when(prompt)
    def _():
        attend([(3 * pairs // 4 + i) % pairs for i in range(pairs // 2)])
        project((3 * quarter, 0), quarter)
        send_rims()
        start(*shared[:2])
        attend([pairs // 4 + i for i in range(pairs // 2)])
        project((quarter,), 2 * quarter)
        start(shared[2])

    taps_copy.wait()
    alpha_copy.wait()
    pick_row = lax.broadcasted_iota(jnp.int32, (half, 2 * half), 0)
    pick_col = lax.broadcasted_iota(jnp.int32, (half, 2 * half), 1)
    picked = pick_col == pick_row + parity * half
    for k in range(4):
        taps_t[pl.ds(k * half, half), :] = taps[k, pl.ds(pl.multiple_of(parity * half, half), half), :]
    rate = jnp.sum(jnp.where(picked, alpha[...], 0.0), axis=1, keepdims=True)

    def rims_arrived():
        pl.when(has_right)(lambda: wait(rightward, leftward))
        pl.when(has_left)(lambda: wait(leftward, rightward))

    pl.when(prompt)(lambda: wait(shared[:3], shared[:3]))
    pl.when(late)(lambda: wait(shared[3:6], shared[3:6]))
    pl.when(leader)(lambda: wait((shared[4], shared[6]), (shared[4], shared[6])))

    own_is_cond = branch_ids[member] == 0
    strength = guidance[member // 2]
    own_weight = jnp.where(own_is_cond, strength, 1.0 - strength)
    par_weight = jnp.where(own_is_cond, 1.0 - strength, strength)
    def frame_of(at):
        return jnp.where(at < frames + 2 * RIM, at, at - lanes) + tm * frames

    def mix(start, rows):
        frame = frame_of(lax.broadcasted_iota(jnp.int32, (rows, 1), 0) + start)
        inside = (frame >= 0) & (frame < total_frames)
        part = pl.ds(start, rows)
        mixed = own_weight * own[part, :].astype(F32) + par_weight * par[part, :].astype(F32)
        guided[part, :] = jnp.where(inside, mixed, 0.0).astype(BF16)
        y_buf[:, part] = nt_dot(taps_t[...], guided[part, :])

    def finish(tiles, results):
        extent_lanes = 128 * len(tiles)
        lane_at = lax.broadcasted_iota(jnp.int32, (8, 128), 1)
        frame_lane = frame_of(jnp.concatenate([lane_at + 128 * t for t in tiles], axis=1))
        kept = (frame_lane >= 0) & (frame_lane < total_frames)

        def ahead(x, count):
            return pltpu.roll(x, (-count) % extent_lanes, 1)

        for c in range(half // 8):
            rate_c = rate[8 * c : 8 * c + 8]
            turn = rate_c * (1.0 / math.pi)
            inverse = 1.0 / rate_c

            def snake(z):
                t = turn * z
                f = t - jnp.round(t)
                u = f * f
                s = SIN2[5]
                for a in (4, 3, 2, 1, 0):
                    s = s * u + SIN2[a]
                return z + (s * u) * inverse

            y = [jnp.concatenate([y_buf[pl.ds(k * half + 8 * c, 8), pl.ds(128 * t, 128)] for t in tiles],
                                 axis=1) for k in range(4)]
            even = jnp.where(kept, y[1] + ahead(y[3], -1), 0.0)
            odd = jnp.where(kept, ahead(y[0], 1) + y[2], 0.0)
            even_p, odd_m = ahead(even, 1), ahead(odd, -1)
            b0, b1, b2, b3, b4, b5 = HALF_BAND
            between_even = (b0 * ahead(even, -1) + b1 * odd_m + b2 * even + b3 * odd
                            + b4 * even_p + b5 * ahead(odd, 1))
            between_odd = (b0 * odd_m + b1 * even + b2 * odd + b3 * even_p
                           + b4 * ahead(odd, 1) + b5 * ahead(even, 2))
            s_even = jnp.where(kept, snake(between_even), 0.0)
            s_odd = jnp.where(kept, snake(between_odd), 0.0)
            l0, l1, l2, l3, l4, l5 = LOW_PASS
            s_even_m, s_odd_m = ahead(s_even, -1), ahead(s_odd, -1)
            s_even_p, s_odd_p = ahead(s_even, 1), ahead(s_odd, 1)
            w_even = (CENTER_TAP * snake(even) + l0 * ahead(s_odd, -2) + l1 * s_even_m + l2 * s_odd_m
                      + l3 * s_even + l4 * s_odd + l5 * s_even_p)
            w_odd = (CENTER_TAP * snake(odd) + l0 * s_even_m + l1 * s_odd_m + l2 * s_even
                     + l3 * s_odd + l4 * s_even_p + l5 * s_odd_p)
            for b in results:
                at = 128 * tiles.index(b)
                wave[pl.ds(8 * c, 8), pl.ds(256 * b, 128)] = w_even[:, at : at + 128]
                wave[pl.ds(8 * c, 8), pl.ds(256 * b + 128, 128)] = w_odd[:, at : at + 128]

        for b in results:
            cols = pl.ds(256 * b, 256)
            out[:, cols] = dot(wave[:, cols].astype(BF16), perm[...]).astype(BF16)


    n_tiles = lanes // 128
    out_tiles = frames // 128

    @pl.when(whole)
    def _():
        rims_arrived()
        mix(0, lanes)
        finish(list(range(n_tiles)), list(range(out_tiles)))

    @pl.when(split)
    def _():
        mix(0, frames)
        finish(list(range(out_tiles)), list(range(1, out_tiles - 1)))
        rims_arrived()
        mix(frames, lanes - frames)
        finish(list(range(out_tiles - 2, n_tiles)) + [0, 1], [out_tiles - 1, 0])


def on_device(hidden_rows, modulation, project_in, project_out, to_vocoder, upsample_taps,
              snake_alpha, guidance, branch_ids):
    n_tm = lax.axis_size("tm")
    _, frames, width = hidden_rows.shape
    cin, cout = upsample_taps.shape[1:]
    half = cout // 2
    extent = LEFT + frames + BLOCK
    held = (frames // PAIR - 1) * PAIR + 256
    groups = width // 128
    lanes = -(-(frames + 2 * RIM) // 128) * 128
    any_spec = pl.BlockSpec(memory_space=pl.ANY)
    smem = pl.BlockSpec(memory_space=pltpu.SMEM)
    return pl.pallas_call(
        functools.partial(kernel, n_tm),
        out_shape=pltpu.VMEM((half, 2 * frames), BF16),
        in_specs=[any_spec] * 7 + [smem] * 2,
        out_specs=pl.BlockSpec(memory_space=pltpu.VMEM),
        scratch_shapes=[
            pltpu.VMEM((extent, width), BF16),
            pltpu.VMEM((extent, width), BF16),
            pltpu.VMEM((3 * width // 256, width, 256), BF16),
            pltpu.VMEM((width, width), BF16),
            pltpu.VMEM((width, cin), BF16),
            pltpu.VMEM((4, cout, cin), BF16),
            pltpu.VMEM((3, width), F32),
            pltpu.VMEM((1, cout), F32),
            pltpu.VMEM((groups, frames, 128), BF16),
            pltpu.VMEM((groups, held, 128), BF16),
            pltpu.VMEM((groups, held, 128), BF16),
            pltpu.VMEM((frames, width), BF16),
            pltpu.VMEM((frames, width), BF16),
            pltpu.VMEM((lanes, cin), BF16),
            pltpu.VMEM((lanes, cin), BF16),
            pltpu.VMEM((lanes, cin), BF16),
            pltpu.VMEM((4 * half, lanes), F32),
            pltpu.VMEM((half, 2 * frames), F32),
            pltpu.VMEM((4 * half, cin), BF16),
            pltpu.VMEM((256, 256), BF16),
            pltpu.SemaphoreType.DMA((4,)),
            pltpu.SemaphoreType.DMA((3 * width // 256,)),
            pltpu.SemaphoreType.DMA((5,)),
            pltpu.SemaphoreType.DMA((9,)),
            pltpu.SemaphoreType.DMA((9,)),
        ],
        compiler_params=pltpu.CompilerParams(
            collective_id=0, has_side_effects=True, vmem_limit_bytes=56 * 1024 * 1024),
        cost_estimate=pl.CostEstimate(
            flops=9_000_000_000, bytes_accessed=12_000_000, transcendentals=3_000_000),
    )(hidden_rows, modulation.transpose(1, 0, 2), project_in, project_out, to_vocoder,
      upsample_taps.transpose(0, 2, 1), snake_alpha[None, :], guidance, branch_ids)


def solution(mesh):
    in_specs = (P("guide", "tm", None), P("guide", None, None), P(), P(), P(), P(), P(), P(), P())
    return jax.shard_map(
        on_device, mesh=mesh, in_specs=in_specs, out_specs=P("guide", "tm"), check_vma=False)
```

```python
import functools
import math

import jax
import jax.numpy as jnp
from jax import lax
from jax.experimental import pallas as pl
from jax.experimental.pallas import tpu as pltpu
from jax.sharding import PartitionSpec as P

HEADS = 16
BLOCK = 48
HALF_BAND = (3.0 / 256.0, -25.0 / 256.0, 150.0 / 256.0, 150.0 / 256.0, -25.0 / 256.0, 3.0 / 256.0)
LOW_PASS = (0.012, -0.06, 0.3, 0.3, -0.06, 0.012)
CENTER_TAP = 0.5
SIN2 = (9.869604202977849, -32.469663586217976, 42.72706432039706,
        -30.100639734504547, 13.048356860034854, -3.3563323291898937)
MASKED = -1e30
MESH = pl.DeviceIdType.MESH
F32 = jnp.float32
BF16 = jnp.bfloat16

PAIR = 2 * BLOCK
LEFT = 2 * BLOCK
RING = 4
RIM = 16


def nt_dot(a, b):
    return lax.dot_general(a, b, (((1,), (1,)), ((), ())), preferred_element_type=F32)


def dot(a, b):
    return jnp.dot(a, b, preferred_element_type=F32)


def kernel(n_tm, hidden, modulation, w_in_hbm, w_out_hbm, w_voc_hbm, taps_hbm, alpha_hbm,
           guidance, branch_ids, out,
           hid, normed, w_in, w_out, w_voc, taps, mod, alpha,
           q_buf, k_buf, v_buf, att, upd, own, par, guided, y_buf, wave, taps_t, perm,
           hid_sem, win_sem, in_sem, send_sem, recv_sem):
    frames = hidden.shape[1]
    width = hidden.shape[2]
    pairs = frames // PAIR
    groups = width // 128
    extent = LEFT + frames + BLOCK
    half = out.shape[0]
    lanes = own.shape[0]
    cin = own.shape[1]
    total_frames = n_tm * frames

    tm = lax.axis_index("tm")
    member = lax.axis_index("guide")
    parity = lax.rem(member, 2)
    other = member + 1 - 2 * parity
    has_left, has_right = tm > 0, tm < n_tm - 1
    deferred = tm == n_tm // 2
    late = deferred | (tm == n_tm // 2 + 1)
    leader = tm == n_tm // 2 - 1
    prompt = jnp.logical_not(late | leader)
    split = deferred | leader
    whole = jnp.logical_not(split)
    eager = lax.rem(tm, RING) == RING - 1
    left_tm, right_tm = jnp.maximum(tm - 1, 0), jnp.minimum(tm + 1, n_tm - 1)
    left, right = (left_tm, member), (right_tm, member)
    partner = (tm, other)
    left_partner, right_partner = (left_tm, other), (right_tm, other)

    barrier = pltpu.get_barrier_semaphore()

    def greet(*devices):
        for device in devices:
            pl.semaphore_signal(barrier, inc=1, device_id=device, device_id_type=MESH)

    greet(partner)
    pl.when(has_left)(lambda: greet(left, left_partner))
    pl.when(has_right)(lambda: greet(right, right_partner))

    def load(src, dst, sem):
        copy = pltpu.make_async_copy(src, dst, sem)
        copy.start()
        return copy

    parts = 4
    part = frames // parts
    hid_copies = [load(hidden.at[0, pl.ds(part * i, part)], hid.at[pl.ds(LEFT + part * i, part)],
                       hid_sem.at[i]) for i in range(parts)]
    mod_copy = load(modulation.at[:, 0], mod, in_sem.at[0])

    def transfer(i, src, dst, device):
        return pltpu.make_async_remote_copy(
            src_ref=src, dst_ref=dst, send_sem=send_sem.at[i], recv_sem=recv_sem.at[i],
            device_id=device, device_id_type=MESH)

    def start(*copies):
        for copy in copies:
            copy.start()

    def wait(sent, received):
        for copy in sent:
            copy.wait_send()
        for copy in received:
            copy.wait_recv()

    to_right = transfer(0, hidden.at[0, pl.ds(frames - LEFT, LEFT)], hid.at[pl.ds(0, LEFT)], right)
    to_left = transfer(1, hidden.at[0, pl.ds(0, BLOCK)], hid.at[pl.ds(LEFT + frames, BLOCK)], left)

    def share_hidden(left_first=False):
        pl.semaphore_wait(
            barrier, 1 + 2 * has_left.astype(jnp.int32) + 2 * has_right.astype(jnp.int32))
        if left_first:
            pl.when(has_left)(lambda: start(to_left))
        pl.when(has_right)(lambda: start(to_right))
        if not left_first:
            pl.when(has_left)(lambda: start(to_left))

    pl.when(eager)(share_hidden)

    def load_weights():
        tiles = w_in.shape[0]
        copies = [load(w_in_hbm.at[:, pl.ds(256 * j, 256)], w_in.at[j], win_sem.at[j])
                  for j in range(tiles)]
        for i, (src, dst) in enumerate(((w_out_hbm, w_out), (w_voc_hbm, w_voc),
                                        (taps_hbm, taps), (alpha_hbm, alpha))):
            copies.append(load(src, dst, in_sem.at[i + 1]))
        return copies[tiles:]

    hid_copies[0].wait()
    wout_copy, wvoc_copy, taps_copy, alpha_copy = load_weights()

    spare = k_buf.shape[1] - extent
    k_buf[:, pl.ds(extent, spare), :] = jnp.zeros((groups, spare, 128), BF16)
    v_buf[:, pl.ds(extent, spare), :] = jnp.zeros((groups, spare, 128), BF16)
    gap = lanes - frames - 2 * RIM

    def clear(start, count):
        own[pl.ds(start, count), :] = jnp.zeros((count, cin), BF16)
        par[pl.ds(start, count), :] = jnp.zeros((count, cin), BF16)

    clear(frames + RIM, gap)

    @pl.when(tm == 0)
    def _():
        hid[pl.ds(0, LEFT), :] = jnp.zeros((LEFT, width), BF16)
        clear(lanes - RIM, RIM)

    @pl.when(tm == n_tm - 1)
    def _():
        hid[pl.ds(LEFT + frames, BLOCK), :] = jnp.zeros((BLOCK, width), BF16)
        clear(frames, RIM)

    row = lax.broadcasted_iota(jnp.int32, (256, 256), 0)
    col = lax.broadcasted_iota(jnp.int32, (256, 256), 1)
    perm[...] = jnp.where(row == (col % 2) * 128 + col // 2, 1.0, 0.0).astype(BF16)

    mod_copy.wait()
    scale_row = 1.0 + mod[0:1, :]
    shift_row = mod[1:2, :]

    def normalise(start, rows):
        x = hid[pl.ds(start, rows), :].astype(F32)
        centered = x - jnp.mean(x, axis=-1, keepdims=True)
        variance = jnp.mean(centered * centered, axis=-1, keepdims=True)
        result = centered * lax.rsqrt(variance + 1e-6) * scale_row + shift_row
        normed[pl.ds(start, rows), :] = result.astype(BF16)

    for i in range(parts):
        if i > 0:
            hid_copies[i].wait()

        def norm_step(j, carry):
            normalise(pl.multiple_of(LEFT + i * part + j * PAIR, PAIR), PAIR)
            return carry

        lax.fori_loop(0, part // PAIR, norm_step, 0)
        if i == 1:
            pl.when(jnp.logical_not(deferred | eager))(share_hidden)

    per = groups // 2
    local = pl.ds(LEFT, frames)

    def arrived(base):
        for j in range(base, base + per):
            pltpu.make_async_copy(w_in.at[j], w_in.at[j], win_sem.at[j]).wait()

    arrived(0)
    for j in range(per):
        acc = dot(normed[local, :], w_in[j]) * (math.log2(math.e) / math.sqrt(width // HEADS))
        acc = acc.astype(BF16)
        q_buf[2 * j] = acc[:, :128]
        q_buf[2 * j + 1] = acc[:, 128:]

    def keys_values(base, buf, tiles):
        for j in tiles:
            acc = dot(normed[local, :], w_in[base + j]).astype(BF16)
            buf[2 * j, local, :] = acc[:, :128]
            buf[2 * j + 1, local, :] = acc[:, 128:]

    arrived(per)
    arrived(2 * per)
    keys_values(per, k_buf, range(per))
    keys_values(2 * per, v_buf, range(per // 2))
    pl.when(deferred)(lambda: share_hidden(True))
    keys_values(2 * per, v_buf, range(per // 2, per))

    span = 256
    low_half = lax.broadcasted_iota(jnp.int32, (PAIR, 128), 1) < 64
    ones = jnp.ones((span, 128), BF16)
    key_at = lax.broadcasted_iota(jnp.int32, (PAIR, span), 1)
    block_at = lax.broadcasted_iota(jnp.int32, (PAIR, span), 0) // BLOCK * BLOCK
    window = (key_at >= block_at) & (key_at < block_at + 4 * BLOCK)

    def bias_of(p):
        usable = window
        if p == 0:
            usable = usable & ((key_at >= LEFT) | (tm > 0))
        if p == pairs - 1:
            usable = usable & ((key_at < LEFT + PAIR) | (tm < n_tm - 1))
        return jnp.where(usable, 0.0, MASKED)

    def attend(members):
        biases = {p: bias_of(p) for p in members}
        steps = [(p, g) for p in members for g in range(groups)]
        scores, raised = {}, {}

        def score(step):
            p, g = step
            q = q_buf[g, pl.ds(p * PAIR, PAIR), :]
            zero = jnp.zeros_like(q)
            q = jnp.concatenate([jnp.where(low_half, q, zero), jnp.where(low_half, zero, q)], axis=0)
            s = dot(q, jnp.transpose(k_buf[g, pl.ds(p * PAIR, span), :]))
            return jnp.concatenate([s[:PAIR] + biases[p], s[PAIR:] + biases[p]], axis=0)

        def raise_to(s):
            return jnp.exp2(s - jnp.max(s, axis=1, keepdims=True)).astype(BF16)

        def combine(step, weights):
            p, g = step
            v = jnp.concatenate([v_buf[g, pl.ds(p * PAIR, span), :], ones], axis=1)
            result = dot(weights, v)
            numer = jnp.where(low_half, result[:PAIR, :128], result[PAIR:, :128])
            denom = jnp.where(low_half, result[:PAIR, 128:], result[PAIR:, 128:])
            att[pl.ds(p * PAIR, PAIR), pl.ds(128 * g, 128)] = (numer / denom).astype(BF16)

        for t in range(len(steps) + 2):
            if t < len(steps):
                scores[t] = score(steps[t])
            if 0 <= t - 1 < len(steps):
                raised[t - 1] = raise_to(scores.pop(t - 1))
            if t >= 2:
                combine(steps[t - 2], raised.pop(t - 2))

    gate_row = mod[2:3, :]

    def project(starts, rows):
        count = rows * len(starts)
        def rows_of(ref, offset=0):
            return jnp.concatenate([ref[pl.ds(s + offset, rows), :] for s in starts], axis=0)
        for c in range(width // 256):
            cols = pl.ds(256 * c, 256)
            mixed = dot(rows_of(att), w_out[:, cols])
            held = jnp.concatenate(
                [hid[pl.ds(LEFT + s, rows), cols] for s in starts], axis=0).astype(F32)
            upd[pl.ds(0, count), cols] = (held + gate_row[:, 256 * c : 256 * c + 256] * mixed).astype(BF16)
        result = dot(upd[pl.ds(0, count), :], w_voc[...]).astype(BF16)
        for at, s in enumerate(starts):
            own[pl.ds(s, rows), :] = result[at * rows : (at + 1) * rows]

    quarter = frames // 4
    last, first = pl.ds(frames - RIM, RIM), pl.ds(0, RIM)
    before, after = pl.ds(lanes - RIM, RIM), pl.ds(frames, RIM)
    rightward = (transfer(2, own.at[last], own.at[before], right),
                 transfer(3, own.at[last], par.at[before], right_partner))
    leftward = (transfer(4, own.at[first], own.at[after], left),
                transfer(5, own.at[first], par.at[after], left_partner))
    shared = [transfer(i, own.at[pl.ds(s, n)], par.at[pl.ds(s, n)], partner)
              for i, s, n in ((6, 3 * quarter, quarter), (7, 0, quarter), (8, quarter, 2 * quarter),
                              (6, PAIR, frames - 2 * PAIR), (7, frames - PAIR, PAIR), (8, 0, PAIR),
                              (6, 0, frames - PAIR))]

    wout_copy.wait()
    wvoc_copy.wait()

    @pl.when(late)
    def _():
        attend([i for i in range(1, pairs - 1)])
        project((PAIR,), frames - 2 * PAIR)
        start(shared[3])

    @pl.when(leader)
    def _():
        attend([i for i in range(2, pairs - 2)])

    pl.when(has_left)(lambda: wait((to_left,), (to_right,)))
    pl.when(has_right)(lambda: wait((to_right,), (to_left,)))
    normalise(0, LEFT)
    normalise(LEFT + frames, BLOCK)
    rim_rows = jnp.concatenate(
        [normed[pl.ds(0, LEFT), :], normed[pl.ds(LEFT + frames, BLOCK), :]], axis=0)

    def rim_keys_values(base, buf):
        for j in range(per):
            acc = dot(rim_rows, w_in[base + j]).astype(BF16)
            for side in range(2):
                part = acc[:, 128 * side : 128 * side + 128]
                buf[2 * j + side, pl.ds(0, LEFT), :] = part[:LEFT]
                buf[2 * j + side, pl.ds(LEFT + frames, BLOCK), :] = part[LEFT:]

    rim_keys_values(per, k_buf)
    rim_keys_values(2 * per, v_buf)

    def send_rims():
        pl.when(has_right)(lambda: start(*rightward))
        pl.when(has_left)(lambda: start(*leftward))

    @pl.when(late)
    def _():
        attend([pairs - 1, 0])
        project((frames - PAIR, 0), PAIR)
        send_rims()
        start(*shared[4:6])

    @pl.when(leader)
    def _():
        attend([pairs - 1])
        project((frames - PAIR,), PAIR)
        pl.when(has_right)(lambda: start(*rightward))
        start(shared[4])
        attend([0, 1, pairs - 2])
        project((0,), frames - PAIR)
        pl.when(has_left)(lambda: start(*leftward))
        start(shared[6])

    @pl.when(prompt)
    def _():
        attend([(3 * pairs // 4 + i) % pairs for i in range(pairs // 2)])
        project((3 * quarter, 0), quarter)
        send_rims()
        start(*shared[:2])
        attend([pairs // 4 + i for i in range(pairs // 2)])
        project((quarter,), 2 * quarter)
        start(shared[2])

    taps_copy.wait()
    alpha_copy.wait()
    pick_row = lax.broadcasted_iota(jnp.int32, (half, 2 * half), 0)
    pick_col = lax.broadcasted_iota(jnp.int32, (half, 2 * half), 1)
    picked = pick_col == pick_row + parity * half
    for k in range(4):
        taps_t[pl.ds(k * half, half), :] = taps[k, pl.ds(pl.multiple_of(parity * half, half), half), :]
    rate = jnp.sum(jnp.where(picked, alpha[...], 0.0), axis=1, keepdims=True)

    def right_rim_arrived():
        pl.when(has_right)(lambda: wait(rightward, leftward))

    def left_rim_arrived():
        pl.when(has_left)(lambda: wait(leftward, rightward))

    def rims_arrived():
        right_rim_arrived()
        left_rim_arrived()

    pl.when(prompt)(lambda: wait(shared[:3], shared[:3]))
    pl.when(late)(lambda: wait(shared[3:6], shared[3:6]))
    pl.when(leader)(lambda: wait((shared[4], shared[6]), (shared[4], shared[6])))

    own_is_cond = branch_ids[member] == 0
    strength = guidance[member // 2]
    own_weight = jnp.where(own_is_cond, strength, 1.0 - strength)
    par_weight = jnp.where(own_is_cond, 1.0 - strength, strength)
    def frame_of(at):
        return jnp.where(at < frames + 2 * RIM, at, at - lanes) + tm * frames

    def mix(start, rows):
        frame = frame_of(lax.broadcasted_iota(jnp.int32, (rows, 1), 0) + start)
        inside = (frame >= 0) & (frame < total_frames)
        part = pl.ds(start, rows)
        mixed = own_weight * own[part, :].astype(F32) + par_weight * par[part, :].astype(F32)
        guided[part, :] = jnp.where(inside, mixed, 0.0).astype(BF16)
        y_buf[:, part] = nt_dot(taps_t[...], guided[part, :])

    def finish(tiles, results):
        extent_lanes = 128 * len(tiles)
        lane_at = lax.broadcasted_iota(jnp.int32, (8, 128), 1)
        frame_lane = frame_of(jnp.concatenate([lane_at + 128 * t for t in tiles], axis=1))
        kept = (frame_lane >= 0) & (frame_lane < total_frames)

        def ahead(x, count):
            return pltpu.roll(x, (-count) % extent_lanes, 1)

        for c in range(half // 8):
            rate_c = rate[8 * c : 8 * c + 8]
            turn = rate_c * (1.0 / math.pi)
            inverse = 1.0 / rate_c

            def snake(z):
                t = turn * z
                f = t - jnp.round(t)
                u = f * f
                s = SIN2[5]
                for a in (4, 3, 2, 1, 0):
                    s = s * u + SIN2[a]
                return z + (s * u) * inverse

            y = [jnp.concatenate([y_buf[pl.ds(k * half + 8 * c, 8), pl.ds(128 * t, 128)] for t in tiles],
                                 axis=1) for k in range(4)]
            even = jnp.where(kept, y[1] + ahead(y[3], -1), 0.0)
            odd = jnp.where(kept, ahead(y[0], 1) + y[2], 0.0)
            even_p, odd_m = ahead(even, 1), ahead(odd, -1)
            b0, b1, b2, b3, b4, b5 = HALF_BAND
            between_even = (b0 * ahead(even, -1) + b1 * odd_m + b2 * even + b3 * odd
                            + b4 * even_p + b5 * ahead(odd, 1))
            between_odd = (b0 * odd_m + b1 * even + b2 * odd + b3 * even_p
                           + b4 * ahead(odd, 1) + b5 * ahead(even, 2))
            s_even = jnp.where(kept, snake(between_even), 0.0)
            s_odd = jnp.where(kept, snake(between_odd), 0.0)
            l0, l1, l2, l3, l4, l5 = LOW_PASS
            s_even_m, s_odd_m = ahead(s_even, -1), ahead(s_odd, -1)
            s_even_p, s_odd_p = ahead(s_even, 1), ahead(s_odd, 1)
            w_even = (CENTER_TAP * snake(even) + l0 * ahead(s_odd, -2) + l1 * s_even_m + l2 * s_odd_m
                      + l3 * s_even + l4 * s_odd + l5 * s_even_p)
            w_odd = (CENTER_TAP * snake(odd) + l0 * s_even_m + l1 * s_odd_m + l2 * s_even
                     + l3 * s_odd + l4 * s_even_p + l5 * s_odd_p)
            for b in results:
                at = 128 * tiles.index(b)
                wave[pl.ds(8 * c, 8), pl.ds(256 * b, 128)] = w_even[:, at : at + 128]
                wave[pl.ds(8 * c, 8), pl.ds(256 * b + 128, 128)] = w_odd[:, at : at + 128]

        for b in results:
            cols = pl.ds(256 * b, 256)
            out[:, cols] = dot(wave[:, cols].astype(BF16), perm[...]).astype(BF16)


    n_tiles = lanes // 128
    out_tiles = frames // 128

    @pl.when(whole)
    def _():
        rims_arrived()
        mix(0, lanes)
        finish(list(range(n_tiles)), list(range(out_tiles)))

    @pl.when(deferred)
    def _():
        right_rim_arrived()
        mix(0, frames + RIM)
        finish(list(range(n_tiles)), list(range(1, out_tiles)))
        left_rim_arrived()
        mix(frames, lanes - frames)
        finish([n_tiles - 1, 0, 1], [0])

    @pl.when(leader)
    def _():
        mix(0, frames)
        finish(list(range(out_tiles)), list(range(1, out_tiles - 1)))
        rims_arrived()
        mix(frames, lanes - frames)
        finish(list(range(out_tiles - 2, n_tiles)) + [0, 1], [out_tiles - 1, 0])


def on_device(hidden_rows, modulation, project_in, project_out, to_vocoder, upsample_taps,
              snake_alpha, guidance, branch_ids):
    n_tm = lax.axis_size("tm")
    _, frames, width = hidden_rows.shape
    cin, cout = upsample_taps.shape[1:]
    half = cout // 2
    extent = LEFT + frames + BLOCK
    held = (frames // PAIR - 1) * PAIR + 256
    groups = width // 128
    lanes = -(-(frames + 2 * RIM) // 128) * 128
    any_spec = pl.BlockSpec(memory_space=pl.ANY)
    smem = pl.BlockSpec(memory_space=pltpu.SMEM)
    return pl.pallas_call(
        functools.partial(kernel, n_tm),
        out_shape=pltpu.VMEM((half, 2 * frames), BF16),
        in_specs=[any_spec] * 7 + [smem] * 2,
        out_specs=pl.BlockSpec(memory_space=pltpu.VMEM),
        scratch_shapes=[
            pltpu.VMEM((extent, width), BF16),
            pltpu.VMEM((extent, width), BF16),
            pltpu.VMEM((3 * width // 256, width, 256), BF16),
            pltpu.VMEM((width, width), BF16),
            pltpu.VMEM((width, cin), BF16),
            pltpu.VMEM((4, cout, cin), BF16),
            pltpu.VMEM((3, width), F32),
            pltpu.VMEM((1, cout), F32),
            pltpu.VMEM((groups, frames, 128), BF16),
            pltpu.VMEM((groups, held, 128), BF16),
            pltpu.VMEM((groups, held, 128), BF16),
            pltpu.VMEM((frames, width), BF16),
            pltpu.VMEM((frames, width), BF16),
            pltpu.VMEM((lanes, cin), BF16),
            pltpu.VMEM((lanes, cin), BF16),
            pltpu.VMEM((lanes, cin), BF16),
            pltpu.VMEM((4 * half, lanes), F32),
            pltpu.VMEM((half, 2 * frames), F32),
            pltpu.VMEM((4 * half, cin), BF16),
            pltpu.VMEM((256, 256), BF16),
            pltpu.SemaphoreType.DMA((4,)),
            pltpu.SemaphoreType.DMA((3 * width // 256,)),
            pltpu.SemaphoreType.DMA((5,)),
            pltpu.SemaphoreType.DMA((9,)),
            pltpu.SemaphoreType.DMA((9,)),
        ],
        compiler_params=pltpu.CompilerParams(
            collective_id=0, has_side_effects=True, vmem_limit_bytes=56 * 1024 * 1024),
        cost_estimate=pl.CostEstimate(
            flops=9_000_000_000, bytes_accessed=12_000_000, transcendentals=3_000_000),
    )(hidden_rows, modulation.transpose(1, 0, 2), project_in, project_out, to_vocoder,
      upsample_taps.transpose(0, 2, 1), snake_alpha[None, :], guidance, branch_ids)


def solution(mesh):
    in_specs = (P("guide", "tm", None), P("guide", None, None), P(), P(), P(), P(), P(), P(), P())
    return jax.shard_map(
        on_device, mesh=mesh, in_specs=in_specs, out_specs=P("guide", "tm"), check_vma=False)
```
